512 devices in a mesh: chan: 32 (over y, x), row: 2 (over core), col: 8 (over z).
Axes of the slice: x: 4, y: 8, z: 8, core: 2. Of those that a mesh axis runs over, the one named last changes fastest.
Arguments:
- voltages: bfloat16 [2, 2048, 16384], P(None, 'chan', ('row', 'col')), may hold values from -6 to 6
- fir_taps: float32 [4, 64], replicated, may hold values from -3 to 3
Outputs:
- visibilities: bfloat16 [2, 64, 2048, 2048], P(None, 'chan', 'row', 'col')
The draws below stay inside these ranges and needn't reach their ends.
All inputs are finite; a program needn't handle non-finite values.
Results may differ from the reference program's by a relative error of at most 0.0057.
Values may be sent and summed in bfloat16 or wider, within the bound.
No kernel may reach another device: no remote copies, remote signals or barrier semaphores. Data moves between devices by JAX's collectives and lax.ppermute only.
A program may use at most 64 MiB of HBM per device.

```python
import math
import jax
import jax.numpy as jnp
from jax import lax

INPUTS = 2048
CHANNELS = 64
TAPS = 4
FRAMES = 256
SAMPLES = 16384


def level_of(rng, shape, cuts, smallest, top_value):
    level, own = 1.0, jax.random.fold_in(rng, 6)
    for dim, parts in cuts:
        draws = jnp.exp(jax.random.uniform(jax.random.fold_in(own, dim), (parts,), jnp.float32, smallest / len(cuts), top_value / len(cuts)))
        level = level * jnp.repeat(draws, shape[dim] // parts).reshape([-1 if axis == dim else 1 for axis in range(len(shape))])
    return level


def scatter_about(key, dims, scale, limit, cuts=(), held_as=jnp.bfloat16):
    entries = scale * jax.random.normal(key, dims, jnp.float32)
    if cuts:
        entries = entries * level_of(key, dims, cuts, -0.22, 0.18)
    return jnp.clip(entries, -limit, limit).astype(held_as)


def setup_inputs(seed: int = 0) -> dict:
    splits = jax.random.split(jax.random.key(seed), 3)
    voltages = scatter_about(splits[0], (2, INPUTS, SAMPLES), 1.0, 6.0, ((1, 32), (2, 16)))
    fir_taps = scatter_about(splits[1], (TAPS, CHANNELS), 0.5, 3.0, (), jnp.float32)
    return {"voltages": voltages, "fir_taps": fir_taps}


def dft_tables(count):
    index = jnp.arange(count, dtype=jnp.int32)
    phase = index[:, None] * index[None, :] % count
    angle = phase.astype(jnp.float32) * (2.0 * math.pi / count)
    cosine = jnp.cos(angle)
    sine_table = jnp.sin(angle)
    top = jnp.concatenate([cosine, -sine_table], 1)
    bottom = jnp.concatenate([sine_table, cosine], 1)
    return jnp.concatenate([top, bottom], 0)

def channelize(block, fir_taps):
    tap_count, channel_count = fir_taps.shape
    framed = block.astype(jnp.float32).reshape(2, block.shape[1], -1, channel_count)
    frame_count = framed.shape[2]
    padded = jnp.concatenate([jnp.zeros((2, block.shape[1], tap_count - 1, channel_count), jnp.float32), framed], 2)
    filtered = jnp.zeros_like(framed)
    for step in range(tap_count):
        filtered = filtered + fir_taps[step] * padded[:, :, tap_count - 1 - step:tap_count - 1 - step + frame_count, :]
    table = dft_tables(channel_count)
    joined = jnp.concatenate([filtered[0], filtered[1]], -1)
    result = jnp.einsum('ifn,nk->kif', joined, table, precision=lax.Precision.HIGHEST) * (1.0 / math.sqrt(channel_count))
    return result.reshape(2, channel_count, block.shape[1], frame_count).astype(jnp.bfloat16)

def reference(voltages, fir_taps):
    block_size = 64
    blocks = voltages.reshape(2, INPUTS // block_size, block_size, SAMPLES).transpose(1, 0, 2, 3)
    spectra = lax.map(lambda block: channelize(block, fir_taps), blocks)
    spectra = spectra.transpose(1, 2, 0, 3, 4).reshape(2, CHANNELS, INPUTS, FRAMES)
    row_ids = jnp.arange(INPUTS, dtype=jnp.int32)
    upper = row_ids[:, None] < row_ids[None, :]
    factor = 1.0 / math.sqrt(FRAMES)

    def correlate(channel_spec):
        real_part = channel_spec[0].astype(jnp.float32)
        imag_part = channel_spec[1].astype(jnp.float32)
        left_side = jnp.concatenate([real_part, imag_part], 1)
        swapped = jnp.concatenate([imag_part, -real_part], 1)
        vis_real = jnp.dot(left_side, left_side.T, preferred_element_type=jnp.float32, precision=lax.Precision.HIGHEST)
        vis_imag = jnp.dot(swapped, left_side.T, preferred_element_type=jnp.float32, precision=lax.Precision.HIGHEST)
        stacked = jnp.stack([vis_real, vis_imag]) * factor
        return jnp.where(upper[None], stacked, 0.0).astype(jnp.bfloat16)
    result = lax.map(correlate, spectra.transpose(1, 0, 2, 3))
    return result.transpose(1, 0, 2, 3)
```

```python
import functools
import math

import jax
import jax.numpy as jnp
import numpy as np
from jax import lax
from jax.experimental import pallas as pl
from jax.experimental.pallas import tpu as pltpu
from jax.sharding import PartitionSpec as P

VMEM_LIMIT = 40 * 1024 * 1024
LANES = 128


def interleaved_table(channels, group):
    index = np.arange(channels)
    angle = (index[:, None] * index[None, :] % channels) * (2.0 * math.pi / channels)
    cosine, sine = np.cos(angle), np.sin(angle)
    dft = np.stack([np.stack([cosine, sine], 1), np.stack([-sine, cosine], 1)], 1)
    dft = dft / math.sqrt(channels)
    table = np.einsum("kopn,tu->kotpun", dft, np.eye(group))
    return table.reshape(channels * 2 * group, 2 * group * channels).astype(np.float32)


def channelize_kernel(volt_ref, halo_ref, taps_ref, table_ref, out_ref):
    inputs, samples = volt_ref.shape[1:]
    channels = taps_ref.shape[1]
    wide = jnp.concatenate([taps_ref[...]] * (LANES // channels), 1)
    taps = jnp.concatenate([wide] * (samples // LANES), 1)
    head = halo_ref.shape[2]
    parts = []
    for part in range(2):
        extended = jnp.concatenate([halo_ref[part], volt_ref[part]], 1).astype(jnp.float32)
        rolled = pltpu.roll(extended, channels, 1)
        parts.append(
            taps[0:1] * extended[:, head:]
            + taps[1:2] * rolled[:, head:]
            + taps[2:3] * extended[:, head - LANES : head - LANES + samples]
            + taps[3:4] * rolled[:, head - LANES : head - LANES + samples]
        )
    width = table_ref.shape[1] // 2
    rows = []
    for start in range(0, samples, width):
        rows.append(
            jnp.concatenate([parts[0][:, start : start + width], parts[1][:, start : start + width]], 1)
        )
    frames = jnp.concatenate(rows, 0)
    spectra = lax.dot_general(
        table_ref[...],
        frames,
        (((1,), (1,)), ((), ())),
        precision=lax.Precision.HIGHEST,
        preferred_element_type=jnp.float32,
    )
    out_ref[...] = spectra.astype(jnp.bfloat16)


def turn_kernel(place_ref, in_ref, keep_ref, give_ref):
    row = place_ref[0]
    pairs = in_ref.shape[1] // 4
    lane = lax.broadcasted_iota(jnp.int32, (8, LANES), 1)
    low = lane < LANES // 2
    for mine, out_ref in ((True, keep_ref), (False, give_ref)):
        half = row if mine else 1 - row
        for pair in range(pairs):
            first = [in_ref[r, half * 2 * pairs + 2 * pair].astype(jnp.float32) for r in range(2)]
            second = [in_ref[r, half * 2 * pairs + 2 * pair + 1].astype(jnp.float32) for r in range(2)]
            pieces = []
            for ch in range(2):
                for g in range(4):
                    for r in range(2):
                        tile = (slice(ch * 8, ch * 8 + 8), slice((g // 2) * LANES, (g // 2 + 1) * LANES))
                        a, b = first[r][tile], second[r][tile]
                        if g % 2 == 0:
                            pieces.append(jnp.where(low, a, pltpu.roll(b, LANES // 2, 1)))
                        else:
                            pieces.append(jnp.where(low, pltpu.roll(a, LANES // 2, 1), b))
            block = jnp.concatenate(pieces, 0)
            out_ref[pl.ds(pair * LANES, LANES), :] = block.T.astype(jnp.bfloat16)


def by_channel(even, odd):
    low = lax.broadcasted_iota(jnp.int32, even.shape, 1) < LANES // 2
    a, b = even.astype(jnp.float32), odd.astype(jnp.float32)
    first = jnp.where(low, a, pltpu.roll(b, LANES // 2, 1))
    second = jnp.where(low, pltpu.roll(a, LANES // 2, 1), b)
    return first.astype(jnp.bfloat16), second.astype(jnp.bfloat16)


def correlate_kernel(scale, place_ref, *refs):
    left_refs, col_refs = refs[:8], refs[8:16]
    out_ref, right_ref = refs[16], refs[17]
    row, col = place_ref[0], place_ref[1]
    tile = pl.program_id(0)
    tile_rows = left_refs[0].shape[0]
    cols = col_refs[0].shape[0]

    @pl.when(tile == 0)
    def _():
        lane = lax.broadcasted_iota(jnp.int32, (cols, LANES), 1)
        real_lane = lane % 8 < 4
        for pair in range(4):
            blocks = by_channel(col_refs[2 * pair][...], col_refs[2 * pair + 1][...])
            for ch in range(2):
                block = blocks[ch]
                wide = block.astype(jnp.float32)
                turned = jnp.where(real_lane, -pltpu.roll(wide, LANES - 4, 1), pltpu.roll(wide, 4, 1))
                right_ref[ch, 0:cols, pair * LANES : (pair + 1) * LANES] = block
                right_ref[ch, cols : 2 * cols, pair * LANES : (pair + 1) * LANES] = turned.astype(jnp.bfloat16)

    lefts = ([], [])
    for pair in range(4):
        blocks = by_channel(left_refs[2 * pair][...], left_refs[2 * pair + 1][...])
        for ch in range(2):
            lefts[ch].append(blocks[ch])
    row_ids = row * (tile_rows * pl.num_programs(0)) + tile * tile_rows + lax.broadcasted_iota(
        jnp.int32, (tile_rows, cols), 0
    )
    col_ids = col * cols + lax.broadcasted_iota(jnp.int32, (tile_rows, cols), 1)
    upper = row_ids < col_ids
    for ch in range(2):
        left = jnp.concatenate(lefts[ch], 1)
        total = lax.dot_general(
            left, right_ref[ch], (((1,), (1,)), ((), ())), preferred_element_type=jnp.float32
        )
        total = total * scale
        out_ref[0, ch] = jnp.where(upper, total[:, :cols], 0.0).astype(jnp.bfloat16)
        out_ref[1, ch] = jnp.where(upper, total[:, cols:], 0.0).astype(jnp.bfloat16)


def shards(voltages, fir_taps):
    inputs_loc, samples = voltages.shape[1:]
    tap_count, channels = fir_taps.shape
    group = 4
    chan_size, row_size, col_size = (lax.axis_size(a) for a in ("chan", "row", "col"))
    row, col = lax.axis_index("row"), lax.axis_index("col")
    place = jnp.stack([row, col]).astype(jnp.int32)
    devices = row_size * col_size
    params = pltpu.CompilerParams(vmem_limit_bytes=VMEM_LIMIT)
    whole = pl.BlockSpec(memory_space=pltpu.VMEM)
    scalar = pl.BlockSpec(memory_space=pltpu.SMEM)

    halo = lax.ppermute(
        voltages[:, :, samples - group * channels :],
        ("row", "col"),
        [(i, i + 1) for i in range(devices - 1)],
    )
    table = jnp.asarray(interleaved_table(channels, group))
    frames_loc = samples // channels
    spectra = pl.pallas_call(
        channelize_kernel,
        out_shape=jax.ShapeDtypeStruct((channels * 2 * group, frames_loc // group * inputs_loc), jnp.bfloat16),
        in_specs=[whole] * 4,
        out_specs=whole,
        compiler_params=params,
        name="channelize",
    )(voltages, halo, fir_taps, table)
    spectra = spectra.reshape(chan_size, -1, spectra.shape[1])
    turned = lax.all_to_all(spectra, "chan", split_axis=0, concat_axis=0, tiled=True)
    both = lax.all_gather(turned, "row", axis=0)

    half = chan_size * inputs_loc // row_size
    keep, give = pl.pallas_call(
        turn_kernel,
        out_shape=[jax.ShapeDtypeStruct((half, LANES), jnp.bfloat16)] * 2,
        in_specs=[scalar, whole],
        out_specs=[whole] * 2,
        compiler_params=params,
        name="turn",
    )(place, both)

    ahead = [(c, (c + 1) % col_size) for c in range(col_size)]
    behind = [(col_size + c, col_size + (c - 1) % col_size) for c in range(col_size)]
    on_ring = lambda array: lax.ppermute(array, ("row", "col"), ahead + behind)
    swap = lambda array: lax.ppermute(array, "row", [(0, 1), (1, 0)])

    cols = chan_size * inputs_loc // col_size
    col_offset = lax.rem(col, col_size // row_size) * cols
    next_offset = lax.rem(col + 1, col_size // row_size) * cols
    keeps, gives, others = [keep], [give], []
    for step in range(col_size // 2 - 1):
        keeps.append(on_ring(keeps[-1]))
        gives.append(on_ring(gives[-1]))
        others.append(swap(gives[-1]))
    last = on_ring(keeps[-1])
    last_col = on_ring(lax.dynamic_slice_in_dim(gives[-1], next_offset, cols, 0))
    col_part = lambda array: lax.dynamic_slice_in_dim(array, col_offset, cols, 0)
    far_cols = swap(jnp.stack([col_part(k) for k in keeps[1:]]))

    lefts = keeps + [last] + others
    elsewhere = (row == 0) & (col >= col_size // row_size)
    own_cols = [col_part(a) for a in lefts]
    other_cols = [col_part(a) for a in gives] + [last_col] + [far_cols[i] for i in range(len(others))]
    col_blocks = [jnp.where(elsewhere, o, m) for m, o in zip(own_cols, other_cols)]

    tile = 256
    out = pl.pallas_call(
        functools.partial(correlate_kernel, 1.0 / math.sqrt(frames_loc * devices)),
        grid=(half // tile,),
        out_shape=jax.ShapeDtypeStruct((2, 2, half, cols), jnp.bfloat16),
        in_specs=[scalar]
        + [pl.BlockSpec((tile, LANES), lambda i: (i, 0))] * 8
        + [pl.BlockSpec((cols, LANES), lambda i: (0, 0))] * 8,
        out_specs=pl.BlockSpec((2, 2, tile, cols), lambda i: (0, 0, i, 0)),
        scratch_shapes=[pltpu.VMEM((2, 2 * cols, 4 * LANES), jnp.bfloat16)],
        compiler_params=params,
        name="correlate",
    )(place, *lefts, *col_blocks)
    return out


def solution(mesh):
    placed = (P(None, "chan", ("row", "col")), P())
    return jax.shard_map(
        shards, mesh=mesh, in_specs=placed, out_specs=P(None, "chan", "row", "col"), check_vma=False
    )
```

```python
import functools
import math

import jax
import jax.numpy as jnp
import numpy as np
from jax import lax
from jax.experimental import pallas as pl
from jax.experimental.pallas import tpu as pltpu
from jax.sharding import PartitionSpec as P

VMEM_LIMIT = 40 * 1024 * 1024
LANES = 128


def interleaved_table(channels, group):
    index = np.arange(channels)
    angle = (index[:, None] * index[None, :] % channels) * (2.0 * math.pi / channels)
    cosine, sine = np.cos(angle), np.sin(angle)
    dft = np.stack([np.stack([cosine, sine], 1), np.stack([-sine, cosine], 1)], 1)
    dft = dft / math.sqrt(channels)
    table = np.einsum("kopn,tu->kotpun", dft, np.eye(group))
    table = table.reshape(channels * 2 * group, 2 * group * channels).astype(np.float32)
    high = table.astype(jnp.bfloat16)
    return high, (table - high.astype(np.float32)).astype(jnp.bfloat16)


def product_nt(a, b):
    return lax.dot_general(a, b, (((1,), (1,)), ((), ())), preferred_element_type=jnp.float32)


def channelize_kernel(volt_ref, halo_ref, taps_ref, high_ref, rest_ref, out_ref):
    inputs, samples = volt_ref.shape[1:]
    channels = taps_ref.shape[1]
    wide = jnp.concatenate([taps_ref[...]] * (LANES // channels), 1)
    taps = jnp.concatenate([wide] * (samples // LANES), 1)
    head = halo_ref.shape[2]
    parts = []
    for part in range(2):
        extended = jnp.concatenate([halo_ref[part], volt_ref[part]], 1).astype(jnp.float32)
        rolled = pltpu.roll(extended, channels, 1)
        parts.append(
            taps[0:1] * extended[:, head:]
            + taps[1:2] * rolled[:, head:]
            + taps[2:3] * extended[:, head - LANES : head - LANES + samples]
            + taps[3:4] * rolled[:, head - LANES : head - LANES + samples]
        )
    width = high_ref.shape[1] // 2
    rows = []
    for start in range(0, samples, width):
        rows.append(
            jnp.concatenate([parts[0][:, start : start + width], parts[1][:, start : start + width]], 1)
        )
    frames = jnp.concatenate(rows, 0)
    frames_high = frames.astype(jnp.bfloat16)
    frames_rest = (frames - frames_high.astype(jnp.float32)).astype(jnp.bfloat16)
    high = high_ref[...]
    spectra = product_nt(high, frames_rest) + product_nt(rest_ref[...], frames_high)
    spectra = spectra + product_nt(high, frames_high)
    out_ref[...] = spectra.astype(jnp.bfloat16)


def turn_kernel(place_ref, in_ref, keep_ref, give_ref):
    row, odd = place_ref[0], place_ref[1] % 2 == 1
    pairs = in_ref.shape[1] // 4
    half_lanes = LANES // 2
    low = lax.broadcasted_iota(jnp.int32, (8, LANES), 1) < half_lanes
    for mine, out_ref in ((True, keep_ref), (False, give_ref)):
        half = row if mine else 1 - row
        for pair in range(pairs):
            first = [in_ref[r, half * 2 * pairs + 2 * pair].astype(jnp.float32) for r in range(2)]
            second = [in_ref[r, half * 2 * pairs + 2 * pair + 1].astype(jnp.float32) for r in range(2)]
            pieces = []
            for ch in range(2):
                for g in range(4):
                    for r in range(2):
                        tile = (slice(ch * 8, ch * 8 + 8), slice((g // 2) * LANES, (g // 2 + 1) * LANES))
                        a, b = first[r][tile], second[r][tile]
                        if g % 2 == 0:
                            pieces.append(jnp.where(low, a, pltpu.roll(b, half_lanes, 1)))
                        else:
                            pieces.append(jnp.where(low, pltpu.roll(a, half_lanes, 1), b))
            count = len(pieces) // 2
            block = jnp.concatenate(
                [jnp.where(odd, pieces[(i + count) % (2 * count)], pieces[i]) for i in range(2 * count)], 0
            )
            out_ref[pl.ds(pair * LANES, LANES), :] = block.T.astype(jnp.bfloat16)


def by_channel(one, other):
    low = lax.broadcasted_iota(jnp.int32, one.shape, 1) < LANES // 2
    return jnp.where(low, one, other), jnp.where(low, other, one)


def correlate_kernel(scale, tile_rows, place_ref, k0, k1, k2, k3, k4, g0, g1, g2, g3, s1, s2, s3, f13, f4, out_ref, right_ref):
    row, col = place_ref[0], place_ref[1]
    away = 1 - row
    cols = out_ref.shape[3]
    tile = pl.program_id(0)
    per_half = k0.shape[0] // cols
    odd = col % 2
    lefts = [
        (lambda at: k0[at, :]), (lambda at: k1[at, :]),
        (lambda at: k2[at, :]), (lambda at: k3[at, :]),
        (lambda at: s2[away, at, :]), (lambda at: s1[away, at, :]),
        (lambda at: k4[at, :]), (lambda at: s3[away, at, :]),
    ]

    @pl.when(tile == 0)
    def _():
        at = pl.ds(pl.multiple_of((col % per_half) * cols, cols), cols)
        elsewhere = (row == 0) & (col >= per_half)
        others = [
            (lambda: g0[at, :]), (lambda: g1[at, :]),
            (lambda: g2[at, :]), (lambda: g3[at, :]),
            (lambda: f13[away, cols : 2 * cols, :]), (lambda: f13[away, 0:cols, :]),
            (lambda: f4[away]), (lambda: f13[away, 2 * cols : 3 * cols, :]),
        ]
        source = lax.broadcasted_iota(jnp.int32, (LANES, LANES), 0)
        target = lax.broadcasted_iota(jnp.int32, (LANES, LANES), 1)
        turn = jnp.where(source == target - 4, (target % 8 >= 4).astype(jnp.float32), 0.0)
        turn = turn - jnp.where(source == target + 4, (target % 8 < 4).astype(jnp.float32), 0.0)
        turn = turn.astype(jnp.bfloat16)
        blocks = [jnp.where(elsewhere, other(), own(at)) for own, other in zip(lefts, others)]
        for pair in range(4):
            lanes = slice(pair * LANES, (pair + 1) * LANES)
            for ch, block in enumerate(by_channel(blocks[2 * pair], blocks[2 * pair + 1])):
                right_ref[ch, 0:cols, lanes] = block
                turned = jnp.dot(block, turn, preferred_element_type=jnp.float32)
                right_ref[ch, cols : 2 * cols, lanes] = turned.astype(jnp.bfloat16)

    at = pl.ds(pl.multiple_of(tile * tile_rows, tile_rows), tile_rows)
    channels = ([], [])
    for pair in range(4):
        for ch, block in enumerate(by_channel(lefts[2 * pair](at), lefts[2 * pair + 1](at))):
            channels[ch].append(block)
    row_ids = row * k0.shape[0] + tile * tile_rows + lax.broadcasted_iota(jnp.int32, (tile_rows, cols), 0)
    col_ids = col * cols + lax.broadcasted_iota(jnp.int32, (tile_rows, cols), 1)
    upper = row_ids < col_ids
    for ch in range(2):
        total = product_nt(jnp.concatenate(channels[ch], 1), right_ref[ch]) * scale
        goes_to = jnp.where(odd == 1, 1 - ch, ch)
        out_ref[0, goes_to] = jnp.where(upper, total[:, :cols], 0.0).astype(jnp.bfloat16)
        out_ref[1, goes_to] = jnp.where(upper, total[:, cols:], 0.0).astype(jnp.bfloat16)


def shards(voltages, fir_taps):
    inputs_loc, samples = voltages.shape[1:]
    channels = fir_taps.shape[1]
    group = 4
    chan_size, row_size, col_size = (lax.axis_size(a) for a in ("chan", "row", "col"))
    row, col = lax.axis_index("row"), lax.axis_index("col")
    place = jnp.stack([row, col]).astype(jnp.int32)
    devices = row_size * col_size
    params = pltpu.CompilerParams(vmem_limit_bytes=VMEM_LIMIT)
    whole = pl.BlockSpec(memory_space=pltpu.VMEM)
    scalar = pl.BlockSpec(memory_space=pltpu.SMEM)

    halo = lax.ppermute(
        voltages[:, :, samples - group * channels :],
        ("row", "col"),
        [(i, i + 1) for i in range(devices - 1)],
    )
    high, rest = interleaved_table(channels, group)
    frames_loc = samples // channels
    spectra_shape = (channels * 2 * group, frames_loc // group * inputs_loc)
    fetched = lambda shape: pl.BlockSpec(shape, lambda i: (0,) * len(shape))
    spectra = pl.pallas_call(
        channelize_kernel,
        grid=(1,),
        out_shape=jax.ShapeDtypeStruct(spectra_shape, jnp.bfloat16),
        in_specs=[fetched(voltages.shape), whole, fetched(fir_taps.shape), fetched(high.shape), fetched(rest.shape)],
        out_specs=fetched(spectra_shape),
        compiler_params=params,
        name="channelize",
    )(voltages, halo, fir_taps, jnp.asarray(high), jnp.asarray(rest))
    spectra = spectra.reshape(chan_size, -1, spectra.shape[1])
    turned = lax.all_to_all(spectra, "chan", split_axis=0, concat_axis=0, tiled=True)
    both = lax.all_gather(turned, "row", axis=0)

    half = chan_size * inputs_loc // row_size
    keep, give = pl.pallas_call(
        turn_kernel,
        out_shape=[jax.ShapeDtypeStruct((half, LANES), jnp.bfloat16)] * 2,
        in_specs=[scalar, whole],
        out_specs=[whole] * 2,
        compiler_params=params,
        name="turn",
    )(place, both)

    ahead = [(c, (c + 1) % col_size) for c in range(col_size)]
    behind = [(col_size + c, col_size + (c - 1) % col_size) for c in range(col_size)]
    on_ring = lambda array: lax.ppermute(array, ("row", "col"), ahead + behind)
    on_chip = lambda array: lax.all_gather(array, "row", axis=0)

    cols = chan_size * inputs_loc // col_size
    col_offset = lax.rem(col, half // cols) * cols
    col_part = lambda array: lax.dynamic_slice_in_dim(array, col_offset, cols, 0)
    keeps, gives = [keep], [give]
    for step in range(col_size // 2 - 1):
        keeps.append(on_ring(keeps[-1]))
        gives.append(on_ring(gives[-1]))
    keeps.append(on_ring(keeps[-1]))
    shared = [on_chip(g) for g in gives[1:]]
    far = on_chip(jnp.concatenate([col_part(k) for k in keeps[1:-1]], 0))
    farthest = on_chip(col_part(keeps[-1]))

    tile = 256
    operands = [*keeps, *gives, *shared, far, farthest]
    return pl.pallas_call(
        functools.partial(correlate_kernel, 1.0 / math.sqrt(frames_loc * devices), tile),
        grid=(half // tile,),
        out_shape=jax.ShapeDtypeStruct((2, 2, half, cols), jnp.bfloat16),
        in_specs=[scalar] + [whole] * len(operands),
        out_specs=pl.BlockSpec((2, 2, tile, cols), lambda i: (0, 0, i, 0)),
        scratch_shapes=[pltpu.VMEM((2, 2 * cols, 4 * LANES), jnp.bfloat16)],
        compiler_params=params,
        name="correlate",
    )(place, *operands)


def solution(mesh):
    placed = (P(None, "chan", ("row", "col")), P())
    return jax.shard_map(
        shards, mesh=mesh, in_specs=placed, out_specs=P(None, "chan", "row", "col"), check_vma=False
    )
```

```python
import functools
import math

import jax
import jax.numpy as jnp
import numpy as np
from jax import lax
from jax.experimental import pallas as pl
from jax.experimental.pallas import tpu as pltpu
from jax.sharding import PartitionSpec as P

VMEM_LIMIT = 40 * 1024 * 1024
WIDE_VMEM_LIMIT = 60 * 1024 * 1024
LANES = 128


def interleaved_table(channels, group):
    index = np.arange(channels)
    angle = (index[:, None] * index[None, :] % channels) * (2.0 * math.pi / channels)
    cosine, sine = np.cos(angle), np.sin(angle)
    dft = np.stack([np.stack([cosine, sine], 1), np.stack([-sine, cosine], 1)], 1)
    dft = dft / math.sqrt(channels)
    table = np.einsum("kopn,tu->kotpun", dft, np.eye(group))
    table = table.reshape(channels * 2 * group, 2 * group * channels).astype(np.float32)
    high = table.astype(jnp.bfloat16)
    return high, (table - high.astype(np.float32)).astype(jnp.bfloat16)


def product_nt(a, b):
    return lax.dot_general(a, b, (((1,), (1,)), ((), ())), preferred_element_type=jnp.float32)


def filtered_groups(extended, taps, head, width):
    samples = extended[0].shape[1] - head
    channels = LANES // 2
    parts = []
    for wide in extended:
        rolled = pltpu.roll(wide, channels, 1)
        parts.append(
            taps[0:1, :samples] * wide[:, head:]
            + taps[1:2, :samples] * rolled[:, head:]
            + taps[2:3, :samples] * wide[:, head - LANES : head - LANES + samples]
            + taps[3:4, :samples] * rolled[:, head - LANES : head - LANES + samples]
        )
    rows = [
        jnp.concatenate([p[:, start : start + width] for p in parts], 1) for start in range(0, samples, width)
    ]
    return jnp.concatenate(rows, 0)


def transformed(frames, high, rest):
    frames_high = frames.astype(jnp.bfloat16)
    frames_rest = (frames - frames_high.astype(jnp.float32)).astype(jnp.bfloat16)
    spectra = product_nt(high, frames_rest) + product_nt(rest, frames_high)
    return (spectra + product_nt(high, frames_high)).astype(jnp.bfloat16)


def later_kernel(
    volt_hbm, taps_hbm, high_hbm, rest_hbm, volt_out, taps_out, high_out, rest_out, late_out, volt_ref, taps_ref, sems
):
    copies = [
        pltpu.make_async_copy(source, target, sems.at[i])
        for i, (source, target) in enumerate(
            ((volt_hbm, volt_ref), (taps_hbm, taps_ref), (high_hbm, high_out), (rest_hbm, rest_out))
        )
    ]
    for copy in copies:
        copy.start()
    copies[0].wait()
    copies[1].wait()
    samples = volt_ref.shape[2]
    wide = jnp.concatenate([taps_ref[...]] * (LANES // taps_ref.shape[1]), 1)
    taps = jnp.concatenate([wide] * (samples // 2 // LANES), 1)
    taps_out[...] = taps
    volt_out[...] = volt_ref[:, :, : samples // 2]
    width = high_out.shape[1] // 2
    extended = [volt_ref[part, :, samples // 2 - width :].astype(jnp.float32) for part in range(2)]
    frames = filtered_groups(extended, taps, width, width)
    copies[2].wait()
    copies[3].wait()
    late_out[...] = transformed(frames, high_out[...], rest_out[...])


def first_kernel(volt_ref, halo_ref, taps_ref, high_ref, rest_ref, late_ref, out_ref):
    extended = [
        jnp.concatenate([halo_ref[part], volt_ref[part]], 1).astype(jnp.float32) for part in range(2)
    ]
    frames = filtered_groups(extended, taps_ref[...], halo_ref.shape[2], high_ref.shape[1] // 2)
    out_ref[:, :LANES] = transformed(frames, high_ref[...], rest_ref[...])
    out_ref[:, LANES:] = late_ref[...]


def turn_kernel(place_ref, in_ref, keep_ref, give_ref):
    row, odd = place_ref[0], place_ref[1] % 2 == 1
    pairs = in_ref.shape[1] // 4
    half_lanes = LANES // 2
    low = lax.broadcasted_iota(jnp.int32, (8, LANES), 1) < half_lanes
    for mine, out_ref in ((True, keep_ref), (False, give_ref)):
        half = row if mine else 1 - row
        for pair in range(pairs):
            first = [in_ref[r, half * 2 * pairs + 2 * pair].astype(jnp.float32) for r in range(2)]
            second = [in_ref[r, half * 2 * pairs + 2 * pair + 1].astype(jnp.float32) for r in range(2)]
            pieces = []
            for ch in range(2):
                for g in range(4):
                    for r in range(2):
                        tile = (slice(ch * 8, ch * 8 + 8), slice((g // 2) * LANES, (g // 2 + 1) * LANES))
                        a, b = first[r][tile], second[r][tile]
                        if g % 2 == 0:
                            pieces.append(jnp.where(low, a, pltpu.roll(b, half_lanes, 1)))
                        else:
                            pieces.append(jnp.where(low, pltpu.roll(a, half_lanes, 1), b))
            count = len(pieces) // 2
            block = jnp.concatenate(
                [jnp.where(odd, pieces[(i + count) % (2 * count)], pieces[i]) for i in range(2 * count)], 0
            )
            out_ref[pl.ds(pair * LANES, LANES), :] = block.T.astype(jnp.bfloat16)


def by_channel(one, other):
    low = lax.broadcasted_iota(jnp.int32, one.shape, 1) < LANES // 2
    return jnp.where(low, one, other), jnp.where(low, other, one)


def correlate_kernel(scale, tile_rows, place_ref, k0, k1, k2, k3, k4, g0, g1, g2, g3, s1, s2, s3, f13, f4, out_ref, right_ref):
    row, col = place_ref[0], place_ref[1]
    away = 1 - row
    cols = out_ref.shape[3]
    tile = pl.program_id(0)
    per_half = k0.shape[0] // cols
    odd = col % 2
    lefts = [
        (lambda at: k0[at, :]), (lambda at: k1[at, :]),
        (lambda at: k2[at, :]), (lambda at: k3[at, :]),
        (lambda at: s2[away, at, :]), (lambda at: s1[away, at, :]),
        (lambda at: k4[at, :]), (lambda at: s3[away, at, :]),
    ]

    @pl.when(tile == 0)
    def _():
        at = pl.ds(pl.multiple_of((col % per_half) * cols, cols), cols)
        elsewhere = (row == 0) & (col >= per_half)
        others = [
            (lambda: g0[at, :]), (lambda: g1[at, :]),
            (lambda: g2[at, :]), (lambda: g3[at, :]),
            (lambda: f13[away, cols : 2 * cols, :]), (lambda: f13[away, 0:cols, :]),
            (lambda: f4[away]), (lambda: f13[away, 2 * cols : 3 * cols, :]),
        ]
        source = lax.broadcasted_iota(jnp.int32, (LANES, LANES), 0)
        target = lax.broadcasted_iota(jnp.int32, (LANES, LANES), 1)
        turn = jnp.where(source == target - 4, (target % 8 >= 4).astype(jnp.float32), 0.0)
        turn = turn - jnp.where(source == target + 4, (target % 8 < 4).astype(jnp.float32), 0.0)
        turn = turn.astype(jnp.bfloat16)
        blocks = [jnp.where(elsewhere, other(), own(at)) for own, other in zip(lefts, others)]
        for pair in range(4):
            lanes = slice(pair * LANES, (pair + 1) * LANES)
            for ch, block in enumerate(by_channel(blocks[2 * pair], blocks[2 * pair + 1])):
                right_ref[ch, 0:cols, lanes] = block
                turned = jnp.dot(block, turn, preferred_element_type=jnp.float32)
                right_ref[ch, cols : 2 * cols, lanes] = turned.astype(jnp.bfloat16)

    at = pl.ds(pl.multiple_of(tile * tile_rows, tile_rows), tile_rows)
    channels = ([], [])
    for pair in range(4):
        for ch, block in enumerate(by_channel(lefts[2 * pair](at), lefts[2 * pair + 1](at))):
            channels[ch].append(block)
    row_ids = row * k0.shape[0] + tile * tile_rows + lax.broadcasted_iota(jnp.int32, (tile_rows, cols), 0)
    col_ids = col * cols + lax.broadcasted_iota(jnp.int32, (tile_rows, cols), 1)
    upper = row_ids < col_ids
    for ch in range(2):
        total = product_nt(jnp.concatenate(channels[ch], 1), right_ref[ch]) * scale
        goes_to = jnp.where(odd == 1, 1 - ch, ch)
        out_ref[0, goes_to] = jnp.where(upper, total[:, :cols], 0.0).astype(jnp.bfloat16)
        out_ref[1, goes_to] = jnp.where(upper, total[:, cols:], 0.0).astype(jnp.bfloat16)


def shards(voltages, fir_taps):
    inputs_loc, samples = voltages.shape[1:]
    channels = fir_taps.shape[1]
    group = 4
    chan_size, row_size, col_size = (lax.axis_size(a) for a in ("chan", "row", "col"))
    row, col = lax.axis_index("row"), lax.axis_index("col")
    place = jnp.stack([row, col]).astype(jnp.int32)
    devices = row_size * col_size
    params = pltpu.CompilerParams(vmem_limit_bytes=VMEM_LIMIT)
    whole = pl.BlockSpec(memory_space=pltpu.VMEM)
    scalar = pl.BlockSpec(memory_space=pltpu.SMEM)

    halo = lax.ppermute(
        voltages[:, :, samples - group * channels :],
        ("row", "col"),
        [(i, i + 1) for i in range(devices - 1)],
    )
    high, rest = interleaved_table(channels, group)
    frames_loc = samples // channels
    spectra_shape = (channels * 2 * group, frames_loc // group * inputs_loc)
    in_hbm = pl.BlockSpec(memory_space=pltpu.HBM)
    like = lambda array: jax.ShapeDtypeStruct(array.shape, array.dtype)
    early = jax.ShapeDtypeStruct((2, inputs_loc, samples // 2), jnp.bfloat16)
    taps_wide = jax.ShapeDtypeStruct((fir_taps.shape[0], samples // 2), jnp.float32)
    late = jax.ShapeDtypeStruct((spectra_shape[0], spectra_shape[1] // 2), jnp.bfloat16)
    volt_early, taps, high, rest, late = pl.pallas_call(
        later_kernel,
        out_shape=[early, taps_wide, like(high), like(rest), late],
        in_specs=[in_hbm] * 4,
        out_specs=[whole] * 5,
        scratch_shapes=[
            pltpu.VMEM(voltages.shape, jnp.bfloat16),
            pltpu.VMEM(fir_taps.shape, jnp.float32),
            pltpu.SemaphoreType.DMA((4,)),
        ],
        cost_estimate=pl.CostEstimate(flops=500_000_000, bytes_accessed=3_000_000, transcendentals=0),
        compiler_params=pltpu.CompilerParams(vmem_limit_bytes=WIDE_VMEM_LIMIT),
        name="later_frames",
    )(voltages, fir_taps, jnp.asarray(high), jnp.asarray(rest))
    spectra = pl.pallas_call(
        first_kernel,
        out_shape=jax.ShapeDtypeStruct(spectra_shape, jnp.bfloat16),
        in_specs=[whole] * 6,
        out_specs=whole,
        compiler_params=params,
        name="first_frames",
    )(volt_early, halo, taps, high, rest, late)
    spectra = spectra.reshape(chan_size, -1, spectra.shape[1])
    turned = lax.all_to_all(spectra, "chan", split_axis=0, concat_axis=0, tiled=True)
    both = lax.all_gather(turned, "row", axis=0)

    half = chan_size * inputs_loc // row_size
    keep, give = pl.pallas_call(
        turn_kernel,
        out_shape=[jax.ShapeDtypeStruct((half, LANES), jnp.bfloat16)] * 2,
        in_specs=[scalar, whole],
        out_specs=[whole] * 2,
        compiler_params=params,
        name="turn",
    )(place, both)

    ahead = [(c, (c + 1) % col_size) for c in range(col_size)]
    behind = [(col_size + c, col_size + (c - 1) % col_size) for c in range(col_size)]
    on_ring = lambda array: lax.ppermute(array, ("row", "col"), ahead + behind)
    on_chip = lambda array: lax.all_gather(array, "row", axis=0)

    cols = chan_size * inputs_loc // col_size
    col_offset = lax.rem(col, half // cols) * cols
    col_part = lambda array: lax.dynamic_slice_in_dim(array, col_offset, cols, 0)
    keeps, gives = [keep], [give]
    for step in range(col_size // 2 - 1):
        keeps.append(on_ring(keeps[-1]))
        gives.append(on_ring(gives[-1]))
    keeps.append(on_ring(keeps[-1]))
    shared = [on_chip(g) for g in gives[1:]]
    far = on_chip(jnp.concatenate([col_part(k) for k in keeps[1:-1]], 0))
    farthest = on_chip(col_part(keeps[-1]))

    tile = 256
    operands = [*keeps, *gives, *shared, far, farthest]
    return pl.pallas_call(
        functools.partial(correlate_kernel, 1.0 / math.sqrt(frames_loc * devices), tile),
        grid=(half // tile,),
        out_shape=jax.ShapeDtypeStruct((2, 2, half, cols), jnp.bfloat16),
        in_specs=[scalar] + [whole] * len(operands),
        out_specs=pl.BlockSpec((2, 2, tile, cols), lambda i: (0, 0, i, 0)),
        scratch_shapes=[pltpu.VMEM((2, 2 * cols, 4 * LANES), jnp.bfloat16)],
        compiler_params=params,
        name="correlate",
    )(place, *operands)


def solution(mesh):
    placed = (P(None, "chan", ("row", "col")), P())
    return jax.shard_map(
        shards, mesh=mesh, in_specs=placed, out_specs=P(None, "chan", "row", "col"), check_vma=False
    )
```

```python
import functools
import math

import jax
import jax.numpy as jnp
import numpy as np
from jax import lax
from jax.experimental import pallas as pl
from jax.experimental.pallas import tpu as pltpu
from jax.sharding import PartitionSpec as P

VMEM_LIMIT = 40 * 1024 * 1024
WIDE_VMEM_LIMIT = 40 * 1024 * 1024
LANES = 128


def interleaved_table(channels, group):
    index = np.arange(channels)
    angle = (index[:, None] * index[None, :] % channels) * (2.0 * math.pi / channels)
    cosine, sine = np.cos(angle), np.sin(angle)
    dft = np.stack([np.stack([cosine, sine], 1), np.stack([-sine, cosine], 1)], 1)
    dft = dft / math.sqrt(channels)
    table = np.einsum("kopn,tu->kotpun", dft, np.eye(group))
    table = table.reshape(channels * 2 * group, 2 * group * channels).astype(np.float32)
    high = table.astype(jnp.bfloat16)
    return high, (table - high.astype(np.float32)).astype(jnp.bfloat16)


def product_nt(a, b):
    return lax.dot_general(a, b, (((1,), (1,)), ((), ())), preferred_element_type=jnp.float32)


def filtered_groups(extended, taps, head, width):
    samples = extended[0].shape[1] - head
    channels = LANES // 2
    parts = []
    for wide in extended:
        rolled = pltpu.roll(wide, channels, 1)
        parts.append(
            taps[0:1, :samples] * wide[:, head:]
            + taps[1:2, :samples] * rolled[:, head:]
            + taps[2:3, :samples] * wide[:, head - LANES : head - LANES + samples]
            + taps[3:4, :samples] * rolled[:, head - LANES : head - LANES + samples]
        )
    rows = [
        jnp.concatenate([p[:, start : start + width] for p in parts], 1) for start in range(0, samples, width)
    ]
    return jnp.concatenate(rows, 0)


def transformed(frames, high, rest):
    frames_high = frames.astype(jnp.bfloat16)
    frames_rest = (frames - frames_high.astype(jnp.float32)).astype(jnp.bfloat16)
    spectra = product_nt(high, frames_rest) + product_nt(rest, frames_high)
    return (spectra + product_nt(high, frames_high)).astype(jnp.bfloat16)


def later_kernel(
    volt_hbm, taps_hbm, high_hbm, rest_hbm, volt_out, taps_out, high_out, rest_out, late_out, volt_ref, taps_ref, sems
):
    copies = [
        pltpu.make_async_copy(source, target, sems.at[i])
        for i, (source, target) in enumerate(
            ((volt_hbm, volt_ref), (taps_hbm, taps_ref), (high_hbm, high_out), (rest_hbm, rest_out))
        )
    ]
    for copy in copies:
        copy.start()
    copies[0].wait()
    copies[1].wait()
    samples = volt_ref.shape[2]
    wide = jnp.concatenate([taps_ref[...]] * (LANES // taps_ref.shape[1]), 1)
    taps = jnp.concatenate([wide] * (samples // 2 // LANES), 1)
    taps_out[...] = taps
    volt_out[...] = volt_ref[:, :, : samples // 2]
    width = high_out.shape[1] // 2
    extended = [volt_ref[part, :, samples // 2 - width :].astype(jnp.float32) for part in range(2)]
    frames = filtered_groups(extended, taps, width, width)
    copies[2].wait()
    copies[3].wait()
    late_out[...] = transformed(frames, high_out[...], rest_out[...])


def first_kernel(volt_ref, halo_ref, taps_ref, high_ref, rest_ref, late_ref, out_ref):
    extended = [
        jnp.concatenate([halo_ref[part], volt_ref[part]], 1).astype(jnp.float32) for part in range(2)
    ]
    frames = filtered_groups(extended, taps_ref[...], halo_ref.shape[2], high_ref.shape[1] // 2)
    out_ref[:, :LANES] = transformed(frames, high_ref[...], rest_ref[...])
    out_ref[:, LANES:] = late_ref[...]


def turn_kernel(place_ref, in_ref, out_ref):
    swapped = (place_ref[0] + place_ref[1]) % 2 == 1
    blocks = out_ref.shape[0] // LANES
    half_lanes = LANES // 2
    low = lax.broadcasted_iota(jnp.int32, (8, LANES), 1) < half_lanes
    for block in range(blocks):
        pieces = []
        for half in range(2):
            source = 4 * (half * blocks + block)
            first = [in_ref[source + r].astype(jnp.float32) for r in range(2)]
            second = [in_ref[source + 2 + r].astype(jnp.float32) for r in range(2)]
            for g in range(4):
                lanes = slice((g // 2) * LANES, (g // 2 + 1) * LANES)
                for r in range(2):
                    a, b = first[r][:, lanes], second[r][:, lanes]
                    if g % 2 == 0:
                        pieces.append(jnp.where(low, a, pltpu.roll(b, half_lanes, 1)))
                    else:
                        pieces.append(jnp.where(low, pltpu.roll(a, half_lanes, 1), b))
        count = len(pieces) // 2
        rows = [jnp.where(swapped, pieces[(i + count) % (2 * count)], pieces[i]) for i in range(2 * count)]
        out_ref[pl.ds(block * LANES, LANES), :] = jnp.concatenate(rows, 0).T.astype(jnp.bfloat16)


def half_of(own, other, flip):
    low = lax.broadcasted_iota(jnp.int32, own.shape, 1) < LANES // 2
    return jnp.where(low != flip, own, other)


def by_channel(one, other):
    low = lax.broadcasted_iota(jnp.int32, one.shape, 1) < LANES // 2
    return jnp.where(low, one, other), jnp.where(low, other, one)


def correlate_kernel(
    scale, tile_rows, place_ref, a0, a1, a2, a3, b0, b1, b2, b3, s1, s2, s3, far, last, out_hbm, out_ref, right_ref, sems
):
    row, col = place_ref[0], place_ref[1]
    away = 1 - row
    cols = out_ref.shape[3]
    half_rows = a0.shape[0]
    per_half = half_rows // cols
    odd = [(col + k) % 2 == 1 for k in range(5)]
    flip_last = (col + row) % 2 == 1
    lefts = [
        (lambda at: half_of(a0[at, :], b0[at, :], odd[0])),
        (lambda at: half_of(a1[at, :], b1[at, :], odd[1])),
        (lambda at: half_of(a2[at, :], b2[at, :], odd[2])),
        (lambda at: half_of(a3[at, :], b3[at, :], odd[3])),
        (lambda at: s2[away, at, :]),
        (lambda at: s1[away, at, :]),
        (lambda at: half_of(last[0, at, :], last[1, at, :], flip_last)),
        (lambda at: s3[away, at, :]),
    ]

    at = pl.ds(pl.multiple_of((col % per_half) * cols, cols), cols)
    elsewhere = (row == 0) & (col >= per_half)
    others = [
        (lambda: half_of(a0[at, :], b0[at, :], ~odd[0])),
        (lambda: half_of(a1[at, :], b1[at, :], ~odd[1])),
        (lambda: half_of(a2[at, :], b2[at, :], ~odd[2])),
        (lambda: half_of(a3[at, :], b3[at, :], ~odd[3])),
        (lambda: far[away, cols : 2 * cols, :]),
        (lambda: far[away, 0:cols, :]),
        (lambda: half_of(last[0, at, :], last[1, at, :], ~flip_last)),
        (lambda: far[away, 2 * cols : 3 * cols, :]),
    ]
    target = lax.broadcasted_iota(jnp.int32, (LANES, LANES), 0)
    source = lax.rem(
        lax.broadcasted_iota(jnp.int32, (LANES, LANES), 1) + jnp.where(elsewhere, LANES // 2, 0), LANES
    )
    same = (source == target).astype(jnp.bfloat16)
    turn = jnp.where(target == source - 4, (source % 8 >= 4).astype(jnp.float32), 0.0)
    turn = turn - jnp.where(target == source + 4, (source % 8 < 4).astype(jnp.float32), 0.0)
    turn = -turn.astype(jnp.bfloat16)
    blocks = [jnp.where(elsewhere, other(), own(at)) for own, other in zip(lefts, others)]
    for pair in range(4):
        lanes = slice(pair * LANES, (pair + 1) * LANES)
        first, second = by_channel(blocks[2 * pair], blocks[2 * pair + 1])
        for ch, block in enumerate((jnp.where(elsewhere, second, first), jnp.where(elsewhere, first, second))):
            right_ref[ch, lanes, 0:cols] = product_nt(same, block).astype(jnp.bfloat16)
            right_ref[ch, lanes, cols : 2 * cols] = product_nt(turn, block).astype(jnp.bfloat16)

    copies = []
    for start in range(0, half_rows, tile_rows):
        here = slice(start, start + tile_rows)
        channels = ([], [])
        for pair in range(4):
            for ch, block in enumerate(by_channel(lefts[2 * pair](here), lefts[2 * pair + 1](here))):
                channels[ch].append(block)
        row_ids = row * half_rows + start + lax.broadcasted_iota(jnp.int32, (tile_rows, cols), 0)
        col_ids = col * cols + lax.broadcasted_iota(jnp.int32, (tile_rows, cols), 1)
        upper = row_ids < col_ids
        for ch in range(2):
            left = jnp.concatenate(channels[ch], 1)
            total = jnp.dot(left, right_ref[ch], preferred_element_type=jnp.float32) * scale
            goes_to = jnp.where(flip_last, 1 - ch, ch)
            out_ref[0, goes_to, here, :] = jnp.where(upper, total[:, :cols], 0.0).astype(jnp.bfloat16)
            out_ref[1, goes_to, here, :] = jnp.where(upper, total[:, cols:], 0.0).astype(jnp.bfloat16)
        copies.append(
            pltpu.make_async_copy(out_ref.at[:, :, here, :], out_hbm.at[:, :, here, :], sems.at[len(copies)])
        )
        copies[-1].start()
    for copy in copies:
        copy.wait()


def shards(voltages, fir_taps):
    inputs_loc, samples = voltages.shape[1:]
    channels = fir_taps.shape[1]
    group = 4
    chan_size, row_size, col_size = (lax.axis_size(a) for a in ("chan", "row", "col"))
    row, col = lax.axis_index("row"), lax.axis_index("col")
    place = jnp.stack([row, col]).astype(jnp.int32)
    devices = row_size * col_size
    params = pltpu.CompilerParams(vmem_limit_bytes=VMEM_LIMIT)
    whole = pl.BlockSpec(memory_space=pltpu.VMEM)
    scalar = pl.BlockSpec(memory_space=pltpu.SMEM)

    halo = lax.ppermute(
        voltages[:, :, samples - group * channels :],
        ("row", "col"),
        [(i, i + 1) for i in range(devices - 1)],
    )
    high, rest = interleaved_table(channels, group)
    frames_loc = samples // channels
    spectra_shape = (channels * 2 * group, frames_loc // group * inputs_loc)
    in_hbm = pl.BlockSpec(memory_space=pltpu.HBM)
    like = lambda array: jax.ShapeDtypeStruct(array.shape, array.dtype)
    early = jax.ShapeDtypeStruct((2, inputs_loc, samples // 2), jnp.bfloat16)
    taps_wide = jax.ShapeDtypeStruct((fir_taps.shape[0], samples // 2), jnp.float32)
    late = jax.ShapeDtypeStruct((spectra_shape[0], spectra_shape[1] // 2), jnp.bfloat16)
    volt_early, taps, high, rest, late = pl.pallas_call(
        later_kernel,
        out_shape=[early, taps_wide, like(high), like(rest), late],
        in_specs=[in_hbm] * 4,
        out_specs=[whole] * 5,
        scratch_shapes=[
            pltpu.VMEM(voltages.shape, jnp.bfloat16),
            pltpu.VMEM(fir_taps.shape, jnp.float32),
            pltpu.SemaphoreType.DMA((4,)),
        ],
        cost_estimate=pl.CostEstimate(flops=500_000_000, bytes_accessed=3_000_000, transcendentals=0),
        compiler_params=pltpu.CompilerParams(vmem_limit_bytes=WIDE_VMEM_LIMIT),
        name="later_frames",
    )(voltages, fir_taps, jnp.asarray(high), jnp.asarray(rest))
    spectra = pl.pallas_call(
        first_kernel,
        out_shape=jax.ShapeDtypeStruct(spectra_shape, jnp.bfloat16),
        in_specs=[whole] * 6,
        out_specs=whole,
        compiler_params=params,
        name="first_frames",
    )(volt_early, halo, taps, high, rest, late)
    spectra = spectra.reshape(chan_size * row_size, -1, spectra.shape[1])
    turned = lax.all_to_all(spectra, ("chan", "row"), split_axis=0, concat_axis=0, tiled=True)

    half = chan_size * inputs_loc // row_size
    own = pl.pallas_call(
        turn_kernel,
        out_shape=jax.ShapeDtypeStruct((half, LANES), jnp.bfloat16),
        in_specs=[scalar, whole],
        out_specs=whole,
        compiler_params=params,
        name="turn",
    )(place, turned)

    ahead = [(c, (c + 1) % col_size) for c in range(col_size)]
    behind = [(col_size + c, col_size + (c - 1) % col_size) for c in range(col_size)]
    on_ring = lambda array: lax.ppermute(array, ("row", "col"), ahead + behind)
    on_chip = lambda array: lax.all_gather(array, "row", axis=0)

    cols = chan_size * inputs_loc // col_size
    col_offset = lax.rem(col, half // cols) * cols
    col_part = lambda array: lax.dynamic_slice_in_dim(array, col_offset, cols, 0)
    owns, others = [own], [lax.dynamic_index_in_dim(on_chip(own), 1 - row, 0, keepdims=False)]
    for step in range(col_size // 2 - 1):
        owns.append(on_ring(owns[-1]))
        others.append(on_ring(others[-1]))
    last = on_chip(on_ring(owns[-1]))
    shared, far = [], []
    for step in range(1, col_size // 2):
        odd = lax.rem(col + step, 2) == 1
        shared.append(on_chip(half_of(owns[step], others[step], ~odd)))
        far.append(half_of(col_part(owns[step]), col_part(others[step]), odd))
    far = on_chip(jnp.concatenate(far, 0))

    tile = 256
    operands = [*owns, *others, *shared, far, last]
    out_shape = (2, 2, half, cols)
    return pl.pallas_call(
        functools.partial(correlate_kernel, 1.0 / math.sqrt(frames_loc * devices), tile),
        out_shape=jax.ShapeDtypeStruct(out_shape, jnp.bfloat16),
        in_specs=[scalar] + [whole] * len(operands),
        out_specs=pl.BlockSpec(memory_space=pl.ANY),
        scratch_shapes=[
            pltpu.VMEM(out_shape, jnp.bfloat16),
            pltpu.VMEM((2, 4 * LANES, 2 * cols), jnp.bfloat16),
            pltpu.SemaphoreType.DMA((half // tile,)),
        ],
        compiler_params=params,
        name="correlate",
    )(place, *operands)


def solution(mesh):
    placed = (P(None, "chan", ("row", "col")), P())
    return jax.shard_map(
        shards, mesh=mesh, in_specs=placed, out_specs=P(None, "chan", "row", "col"), check_vma=False
    )
```

```python
import functools
import math

import jax
import jax.numpy as jnp
import numpy as np
from jax import lax
from jax.experimental import pallas as pl
from jax.experimental.pallas import tpu as pltpu
from jax.sharding import PartitionSpec as P

VMEM_LIMIT = 40 * 1024 * 1024
LANES = 128


def interleaved_table(channels, group):
    index = np.arange(channels)
    angle = (index[:, None] * index[None, :] % channels) * (2.0 * math.pi / channels)
    cosine, sine = np.cos(angle), np.sin(angle)
    dft = np.stack([np.stack([cosine, sine], 1), np.stack([-sine, cosine], 1)], 1)
    dft = dft / math.sqrt(channels)
    table = np.einsum("kopn,tu->kotpun", dft, np.eye(group))
    table = table.reshape(channels * 2 * group, 2 * group * channels).astype(np.float32)
    high = table.astype(jnp.bfloat16)
    return high, (table - high.astype(np.float32)).astype(jnp.bfloat16)


def product_nt(a, b):
    return lax.dot_general(a, b, (((1,), (1,)), ((), ())), preferred_element_type=jnp.float32)


def filtered_groups(extended, taps, head, width):
    samples = extended[0].shape[1] - head
    channels = LANES // 2
    parts = []
    for wide in extended:
        rolled = pltpu.roll(wide, channels, 1)
        parts.append(
            taps[0:1, :samples] * wide[:, head:]
            + taps[1:2, :samples] * rolled[:, head:]
            + taps[2:3, :samples] * wide[:, head - LANES : head - LANES + samples]
            + taps[3:4, :samples] * rolled[:, head - LANES : head - LANES + samples]
        )
    rows = [
        jnp.concatenate([p[:, start : start + width] for p in parts], 1) for start in range(0, samples, width)
    ]
    return jnp.concatenate(rows, 0)


def transformed(frames, high, rest):
    frames_high = frames.astype(jnp.bfloat16)
    frames_rest = (frames - frames_high.astype(jnp.float32)).astype(jnp.bfloat16)
    spectra = product_nt(high, frames_rest) + product_nt(rest, frames_high)
    return (spectra + product_nt(high, frames_high)).astype(jnp.bfloat16)


def later_kernel(volt_hbm, taps_hbm, table_hbm, volt_out, taps_out, table_out, late_out, volt_ref, taps_ref, sems):
    copies = [
        pltpu.make_async_copy(source, target, sems.at[i])
        for i, (source, target) in enumerate(
            ((volt_hbm, volt_ref), (taps_hbm, taps_ref), (table_hbm, table_out))
        )
    ]
    for copy in copies:
        copy.start()
    copies[0].wait()
    copies[1].wait()
    samples = volt_ref.shape[2]
    width = table_out.shape[2] // 2
    wide = jnp.concatenate([taps_ref[...]] * (LANES // taps_ref.shape[1]), 1)
    taps = jnp.concatenate([wide] * (samples // LANES), 1)
    taps_out[...] = taps[:, :width]
    volt_out[...] = volt_ref[:, :, :width]
    extended = [volt_ref[part].astype(jnp.float32) for part in range(2)]
    frames = filtered_groups(extended, taps, width, width)
    first = jnp.zeros((volt_ref.shape[1], frames.shape[1]), jnp.float32)
    copies[2].wait()
    late_out[...] = transformed(jnp.concatenate([first, frames], 0), table_out[0], table_out[1])


def first_kernel(volt_ref, halo_ref, taps_ref, table_ref, late_ref, out_ref):
    extended = [
        jnp.concatenate([halo_ref[part], volt_ref[part]], 1).astype(jnp.float32) for part in range(2)
    ]
    frames = filtered_groups(extended, taps_ref[...], halo_ref.shape[2], table_ref.shape[2] // 2)
    frames = jnp.concatenate([frames, jnp.zeros((LANES - frames.shape[0], frames.shape[1]), jnp.float32)], 0)
    first = transformed(frames, table_ref[0], table_ref[1])
    out_ref[:, :LANES] = first + late_ref[:, :LANES]
    out_ref[:, LANES:] = late_ref[:, LANES:]


def turn_kernel(in_ref, *out_refs):
    row, odd = lax.axis_index("row"), lax.axis_index("col") % 2 == 1
    pairs = in_ref.shape[1] // 4
    half_lanes = LANES // 2
    low = lax.broadcasted_iota(jnp.int32, (8, LANES), 1) < half_lanes
    for half, out_ref in zip((row, 1 - row), out_refs):
        for pair in range(pairs):
            first = [in_ref[r, half * 2 * pairs + 2 * pair].astype(jnp.float32) for r in range(2)]
            second = [in_ref[r, half * 2 * pairs + 2 * pair + 1].astype(jnp.float32) for r in range(2)]
            pieces = []
            for ch in range(2):
                for g in range(4):
                    for r in range(2):
                        tile = (slice(ch * 8, ch * 8 + 8), slice((g // 2) * LANES, (g // 2 + 1) * LANES))
                        a, b = first[r][tile], second[r][tile]
                        if g % 2 == 0:
                            pieces.append(jnp.where(low, a, pltpu.roll(b, half_lanes, 1)))
                        else:
                            pieces.append(jnp.where(low, pltpu.roll(a, half_lanes, 1), b))
            count = len(pieces) // 2
            block = jnp.concatenate(
                [jnp.where(odd, pieces[(i + count) % (2 * count)], pieces[i]) for i in range(2 * count)], 0
            )
            out_ref[pl.ds(pair * LANES, LANES), :] = block.T.astype(jnp.bfloat16)


def by_channel(one, other):
    low = lax.broadcasted_iota(jnp.int32, one.shape, 1) < LANES // 2
    return jnp.where(low, one, other), jnp.where(low, other, one)


def correlate_kernel(
    scale, tile_rows, k0, k1, k2, k3, k4, g0, g1, g2, g3, s1, s2, s3, far, c4, out_hbm, out_ref, right_ref, sems
):
    row, col = lax.axis_index("row"), lax.axis_index("col")
    away = 1 - row
    cols = out_ref.shape[3]
    half_rows = k0.shape[0]
    per_half = half_rows // cols
    odd = col % 2 == 1
    lefts = [
        (lambda at: k0[at, :]),
        (lambda at: k1[at, :]),
        (lambda at: k2[at, :]),
        (lambda at: k3[at, :]),
        (lambda at: s2[away, at, :]),
        (lambda at: s1[away, at, :]),
        (lambda at: k4[at, :]),
        (lambda at: s3[away, at, :]),
    ]

    at = pl.ds(pl.multiple_of((col % per_half) * cols, cols), cols)
    elsewhere = (row == 0) & (col >= per_half)
    others = [
        (lambda: g0[at, :]),
        (lambda: g1[at, :]),
        (lambda: g2[at, :]),
        (lambda: g3[at, :]),
        (lambda: far[away, cols : 2 * cols, :]),
        (lambda: far[away, 0:cols, :]),
        (lambda: c4[away]),
        (lambda: far[away, 2 * cols : 3 * cols, :]),
    ]
    target = lax.broadcasted_iota(jnp.int32, (LANES, LANES), 0)
    source = lax.broadcasted_iota(jnp.int32, (LANES, LANES), 1)
    same = (source == target).astype(jnp.bfloat16)
    turn = jnp.where(target == source + 4, 1.0, 0.0) * (source % 8 < 4).astype(jnp.float32)
    turn = turn - jnp.where(target == source - 4, 1.0, 0.0) * (source % 8 >= 4).astype(jnp.float32)
    turn = turn.astype(jnp.bfloat16)
    blocks = [jnp.where(elsewhere, other(), own(at)) for own, other in zip(lefts, others)]
    for pair in range(4):
        lanes = slice(pair * LANES, (pair + 1) * LANES)
        for ch, block in enumerate(by_channel(blocks[2 * pair], blocks[2 * pair + 1])):
            right_ref[ch, lanes, 0:cols] = product_nt(same, block).astype(jnp.bfloat16)
            right_ref[ch, lanes, cols : 2 * cols] = product_nt(turn, block).astype(jnp.bfloat16)

    copies = []
    for start in range(0, half_rows, tile_rows):
        here = slice(start, start + tile_rows)
        channels = ([], [])
        for pair in range(4):
            for ch, block in enumerate(by_channel(lefts[2 * pair](here), lefts[2 * pair + 1](here))):
                channels[ch].append(block)
        row_ids = row * half_rows + start + lax.broadcasted_iota(jnp.int32, (tile_rows, cols), 0)
        col_ids = col * cols + lax.broadcasted_iota(jnp.int32, (tile_rows, cols), 1)
        upper = row_ids < col_ids
        for ch in range(2):
            left = jnp.concatenate(channels[ch], 1)
            total = jnp.dot(left, right_ref[ch], preferred_element_type=jnp.float32) * scale
            goes_to = jnp.where(odd, 1 - ch, ch)
            out_ref[0, goes_to, here, :] = jnp.where(upper, total[:, :cols], 0.0).astype(jnp.bfloat16)
            out_ref[1, goes_to, here, :] = jnp.where(upper, total[:, cols:], 0.0).astype(jnp.bfloat16)
        copies.append(
            pltpu.make_async_copy(out_ref.at[:, :, here, :], out_hbm.at[:, :, here, :], sems.at[len(copies)])
        )
        copies[-1].start()
    for copy in copies:
        copy.wait()


def shards(voltages, fir_taps):
    inputs_loc, samples = voltages.shape[1:]
    channels = fir_taps.shape[1]
    group = 4
    chan_size, row_size, col_size = (lax.axis_size(a) for a in ("chan", "row", "col"))
    row, col = lax.axis_index("row"), lax.axis_index("col")
    devices = row_size * col_size
    params = pltpu.CompilerParams(vmem_limit_bytes=VMEM_LIMIT)
    whole = pl.BlockSpec(memory_space=pltpu.VMEM)

    halo = lax.ppermute(
        voltages[:, :, samples - group * channels :],
        ("row", "col"),
        [(i, i + 1) for i in range(devices - 1)],
    )
    table = np.stack(interleaved_table(channels, group))
    frames_loc = samples // channels
    spectra_shape = (channels * 2 * group, frames_loc // group * inputs_loc)
    in_hbm = pl.BlockSpec(memory_space=pltpu.HBM)
    volt_early, taps, table, late = pl.pallas_call(
        later_kernel,
        out_shape=[
            jax.ShapeDtypeStruct((2, inputs_loc, group * channels), jnp.bfloat16),
            jax.ShapeDtypeStruct((fir_taps.shape[0], group * channels), jnp.float32),
            jax.ShapeDtypeStruct(table.shape, jnp.bfloat16),
            jax.ShapeDtypeStruct(spectra_shape, jnp.bfloat16),
        ],
        in_specs=[in_hbm] * 3,
        out_specs=[whole] * 4,
        scratch_shapes=[
            pltpu.VMEM(voltages.shape, jnp.bfloat16),
            pltpu.VMEM(fir_taps.shape, jnp.float32),
            pltpu.SemaphoreType.DMA((3,)),
        ],
        cost_estimate=pl.CostEstimate(flops=500_000_000, bytes_accessed=3_000_000, transcendentals=0),
        compiler_params=params,
        name="later_frames",
    )(voltages, fir_taps, jnp.asarray(table))
    spectra = pl.pallas_call(
        first_kernel,
        out_shape=jax.ShapeDtypeStruct(spectra_shape, jnp.bfloat16),
        in_specs=[whole] * 5,
        out_specs=whole,
        compiler_params=params,
        name="first_frames",
    )(volt_early, halo, taps, table, late)
    spectra = spectra.reshape(chan_size, -1, spectra.shape[1])
    turned = lax.all_to_all(spectra, "chan", split_axis=0, concat_axis=0, tiled=True)
    both = lax.all_gather(turned, "row", axis=0)

    half = chan_size * inputs_loc // row_size
    keep, give = pl.pallas_call(
        turn_kernel,
        out_shape=[jax.ShapeDtypeStruct((half, LANES), jnp.bfloat16)] * 2,
        in_specs=[whole],
        out_specs=[whole] * 2,
        compiler_params=params,
        name="turn",
    )(both)

    ahead = [(c, (c + 1) % col_size) for c in range(col_size)]
    behind = [(col_size + c, col_size + (c - 1) % col_size) for c in range(col_size)]
    on_ring = lambda array: lax.ppermute(array, ("row", "col"), ahead + behind)
    on_chip = lambda array: lax.all_gather(array, "row", axis=0)

    cols = chan_size * inputs_loc // col_size
    col_offset = lax.rem(col, half // cols) * cols
    col_part = lambda array: lax.dynamic_slice_in_dim(array, col_offset, cols, 0)
    keeps, gives = [keep], [give]
    for step in range(col_size // 2 - 1):
        keeps.append(on_ring(keeps[-1]))
        gives.append(on_ring(gives[-1]))
    keeps.append(on_ring(keeps[-1]))
    shared = [on_chip(g) for g in gives[1:]]
    far = on_chip(jnp.concatenate([col_part(k) for k in keeps[1:-1]], 0))
    last_cols = on_chip(col_part(keeps[-1]))

    tile = 256
    operands = [*keeps, *gives, *shared, far, last_cols]
    out_shape = (2, 2, half, cols)
    return pl.pallas_call(
        functools.partial(correlate_kernel, 1.0 / math.sqrt(frames_loc * devices), tile),
        out_shape=jax.ShapeDtypeStruct(out_shape, jnp.bfloat16),
        in_specs=[whole] * len(operands),
        out_specs=pl.BlockSpec(memory_space=pl.ANY),
        scratch_shapes=[
            pltpu.VMEM(out_shape, jnp.bfloat16),
            pltpu.VMEM((2, 4 * LANES, 2 * cols), jnp.bfloat16),
            pltpu.SemaphoreType.DMA((half // tile,)),
        ],
        compiler_params=params,
        name="correlate",
    )(*operands)


def solution(mesh):
    placed = (P(None, "chan", ("row", "col")), P())
    return jax.shard_map(
        shards, mesh=mesh, in_specs=placed, out_specs=P(None, "chan", "row", "col"), check_vma=False
    )
```

```python
import functools
import math

import jax
import jax.numpy as jnp
import numpy as np
from jax import lax
from jax.experimental import pallas as pl
from jax.experimental.pallas import tpu as pltpu
from jax.sharding import PartitionSpec as P

VMEM_LIMIT = 40 * 1024 * 1024
LANES = 128
NEAR_FLOPS = 4_000_000_000


def interleaved_table(channels, group):
    index = np.arange(channels)
    angle = (index[:, None] * index[None, :] % channels) * (2.0 * math.pi / channels)
    cosine, sine = np.cos(angle), np.sin(angle)
    dft = np.stack([np.stack([cosine, sine], 1), np.stack([-sine, cosine], 1)], 1)
    dft = dft / math.sqrt(channels)
    table = np.einsum("kopn,tu->kotpun", dft, np.eye(group))
    table = table.reshape(channels * 2 * group, 2 * group * channels).astype(np.float32)
    high = table.astype(jnp.bfloat16)
    return high, (table - high.astype(np.float32)).astype(jnp.bfloat16)


def product_nt(a, b):
    return lax.dot_general(a, b, (((1,), (1,)), ((), ())), preferred_element_type=jnp.float32)


def filtered_groups(extended, taps, head, width):
    samples = extended[0].shape[1] - head
    channels = LANES // 2
    parts = []
    for wide in extended:
        rolled = pltpu.roll(wide, channels, 1)
        parts.append(
            taps[0:1, :samples] * wide[:, head:]
            + taps[1:2, :samples] * rolled[:, head:]
            + taps[2:3, :samples] * wide[:, head - LANES : head - LANES + samples]
            + taps[3:4, :samples] * rolled[:, head - LANES : head - LANES + samples]
        )
    rows = [
        jnp.concatenate([p[:, start : start + width] for p in parts], 1) for start in range(0, samples, width)
    ]
    return jnp.concatenate(rows, 0)


def transformed(frames, high, rest):
    frames_high = frames.astype(jnp.bfloat16)
    frames_rest = (frames - frames_high.astype(jnp.float32)).astype(jnp.bfloat16)
    spectra = product_nt(high, frames_rest) + product_nt(rest, frames_high)
    return (spectra + product_nt(high, frames_high)).astype(jnp.bfloat16)


def later_kernel(volt_hbm, taps_hbm, table_hbm, volt_out, taps_out, table_out, late_out, volt_ref, taps_ref, sems):
    copies = [
        pltpu.make_async_copy(source, target, sems.at[i])
        for i, (source, target) in enumerate(
            ((volt_hbm, volt_ref), (taps_hbm, taps_ref), (table_hbm, table_out))
        )
    ]
    for copy in copies:
        copy.start()
    copies[0].wait()
    copies[1].wait()
    samples = volt_ref.shape[2]
    width = table_out.shape[2] // 2
    wide = jnp.concatenate([taps_ref[...]] * (LANES // taps_ref.shape[1]), 1)
    taps = jnp.concatenate([wide] * (samples // LANES), 1)
    taps_out[...] = taps[:, :width]
    volt_out[...] = volt_ref[:, :, :width]
    extended = [volt_ref[part].astype(jnp.float32) for part in range(2)]
    frames = filtered_groups(extended, taps, width, width)
    first = jnp.zeros((volt_ref.shape[1], frames.shape[1]), jnp.float32)
    copies[2].wait()
    late_out[...] = transformed(jnp.concatenate([first, frames], 0), table_out[0], table_out[1])


def first_kernel(volt_ref, halo_ref, taps_ref, table_ref, late_ref, out_ref):
    extended = [
        jnp.concatenate([halo_ref[part], volt_ref[part]], 1).astype(jnp.float32) for part in range(2)
    ]
    frames = filtered_groups(extended, taps_ref[...], halo_ref.shape[2], table_ref.shape[2] // 2)
    frames = jnp.concatenate([frames, jnp.zeros((LANES - frames.shape[0], frames.shape[1]), jnp.float32)], 0)
    first = transformed(frames, table_ref[0], table_ref[1])
    out_ref[:, :LANES] = first + late_ref[:, :LANES]
    out_ref[:, LANES:] = late_ref[:, LANES:]


def turn_kernel(in_ref, *out_refs):
    row, odd = lax.axis_index("row"), lax.axis_index("col") % 2 == 1
    pairs = in_ref.shape[1] // 4
    half_lanes = LANES // 2
    low = lax.broadcasted_iota(jnp.int32, (8, LANES), 1) < half_lanes
    for half, out_ref in zip((row, 1 - row), out_refs):
        for pair in range(pairs):
            first = [in_ref[r, half * 2 * pairs + 2 * pair].astype(jnp.float32) for r in range(2)]
            second = [in_ref[r, half * 2 * pairs + 2 * pair + 1].astype(jnp.float32) for r in range(2)]
            pieces = []
            for ch in range(2):
                for g in range(4):
                    for r in range(2):
                        tile = (slice(ch * 8, ch * 8 + 8), slice((g // 2) * LANES, (g // 2 + 1) * LANES))
                        a, b = first[r][tile], second[r][tile]
                        if g % 2 == 0:
                            pieces.append(jnp.where(low, a, pltpu.roll(b, half_lanes, 1)))
                        else:
                            pieces.append(jnp.where(low, pltpu.roll(a, half_lanes, 1), b))
            count = len(pieces) // 2
            block = jnp.concatenate(
                [jnp.where(odd, pieces[(i + count) % (2 * count)], pieces[i]) for i in range(2 * count)], 0
            )
            out_ref[pl.ds(pair * LANES, LANES), :] = block.T.astype(jnp.bfloat16)


def by_channel(one, other):
    low = lax.broadcasted_iota(jnp.int32, one.shape, 1) < LANES // 2
    return jnp.where(low, one, other), jnp.where(low, other, one)


def place_of_columns(cols, half_rows):
    row, col = lax.axis_index("row"), lax.axis_index("col")
    per_half = half_rows // cols
    at = pl.ds(pl.multiple_of((col % per_half) * cols, cols), cols)
    return row, col, at, (row == 0) & (col >= per_half)


def put_columns(one, other, right_ref, first_lane):
    cols = one.shape[0]
    target = lax.broadcasted_iota(jnp.int32, (LANES, LANES), 0)
    source = lax.broadcasted_iota(jnp.int32, (LANES, LANES), 1)
    same = (source == target).astype(jnp.bfloat16)
    turn = jnp.where(target == source + 4, 1.0, 0.0) * (source % 8 < 4).astype(jnp.float32)
    turn = turn - jnp.where(target == source - 4, 1.0, 0.0) * (source % 8 >= 4).astype(jnp.float32)
    turn = turn.astype(jnp.bfloat16)
    lanes = slice(first_lane, first_lane + LANES)
    for ch, block in enumerate(by_channel(one, other)):
        right_ref[ch, lanes, 0:cols] = product_nt(same, block).astype(jnp.bfloat16)
        right_ref[ch, lanes, cols : 2 * cols] = product_nt(turn, block).astype(jnp.bfloat16)


def near_columns_kernel(k0, k1, k2, k3, g0, g1, g2, g3, right_ref):
    _, _, at, elsewhere = place_of_columns(right_ref.shape[2] // 2, k0.shape[0])
    near = [jnp.where(elsewhere, g[at, :], k[at, :]) for k, g in ((k0, g0), (k1, g1), (k2, g2), (k3, g3))]
    put_columns(near[0], near[1], right_ref, 0)
    put_columns(near[2], near[3], right_ref, LANES)


def correlate_kernel(
    scale, tile_rows, k0, k1, k2, k3, k4, near, s1, s2, s3, far, out_hbm, out_ref, right_ref, sems
):
    cols = out_ref.shape[3]
    half_rows = k0.shape[0]
    row, col, at, elsewhere = place_of_columns(cols, half_rows)
    away = 1 - row
    odd = col % 2 == 1
    lefts = [
        (lambda at: k0[at, :]),
        (lambda at: k1[at, :]),
        (lambda at: k2[at, :]),
        (lambda at: k3[at, :]),
        (lambda at: s2[away, at, :]),
        (lambda at: s1[away, at, :]),
        (lambda at: k4[at, :]),
        (lambda at: s3[away, at, :]),
    ]

    def prepare():
        theirs = [far[cols * n : cols * (n + 1), :] for n in (1, 0, 3, 2)]
        blocks = [jnp.where(elsewhere, other, own(at)) for own, other in zip(lefts[4:], theirs)]
        put_columns(blocks[0], blocks[1], right_ref, 0)
        put_columns(blocks[2], blocks[3], right_ref, LANES)

    def copy_of(start):
        here = slice(start, start + tile_rows)
        return pltpu.make_async_copy(
            out_ref.at[:, :, here, :], out_hbm.at[:, :, here, :], sems.at[start // tile_rows]
        )

    def products(start):
        here = slice(start, start + tile_rows)
        channels = ([], [])
        for pair in range(4):
            for ch, block in enumerate(by_channel(lefts[2 * pair](here), lefts[2 * pair + 1](here))):
                channels[ch].append(block)
        row_ids = row * half_rows + start + lax.broadcasted_iota(jnp.int32, (tile_rows, cols), 0)
        col_ids = col * cols + lax.broadcasted_iota(jnp.int32, (tile_rows, cols), 1)
        upper = row_ids < col_ids
        for ch in range(2):
            left = jnp.concatenate(channels[ch], 1)
            total = jnp.dot(left[:, : 2 * LANES], near[ch], preferred_element_type=jnp.float32)
            total = total + jnp.dot(left[:, 2 * LANES :], right_ref[ch], preferred_element_type=jnp.float32)
            total = total * scale
            goes_to = jnp.where(odd, 1 - ch, ch)
            out_ref[0, goes_to, here, :] = jnp.where(upper, total[:, :cols], 0.0).astype(jnp.bfloat16)
            out_ref[1, goes_to, here, :] = jnp.where(upper, total[:, cols:], 0.0).astype(jnp.bfloat16)
        copy_of(start).start()

    starts = range(0, half_rows, tile_rows)
    reach = (col + 1) * cols - row * half_rows

    @pl.when(reach >= half_rows)
    def _():
        prepare()
        for start in starts:
            products(start)

    @pl.when(reach < half_rows)
    def _():
        for start in starts:

            @pl.when(reach <= start)
            def _():
                here = slice(start, start + tile_rows)
                out_ref[:, :, here, :] = jnp.zeros((2, 2, tile_rows, cols), jnp.bfloat16)
                copy_of(start).start()

        @pl.when(reach > 0)
        def _():
            prepare()

        for start in starts:
            pl.when(reach > start)(functools.partial(products, start))

    for start in starts:
        copy_of(start).wait()


def shards(voltages, fir_taps):
    inputs_loc, samples = voltages.shape[1:]
    channels = fir_taps.shape[1]
    group = 4
    chan_size, row_size, col_size = (lax.axis_size(a) for a in ("chan", "row", "col"))
    row, col = lax.axis_index("row"), lax.axis_index("col")
    devices = row_size * col_size
    params = pltpu.CompilerParams(vmem_limit_bytes=VMEM_LIMIT)
    whole = pl.BlockSpec(memory_space=pltpu.VMEM)

    halo = lax.ppermute(
        voltages[:, :, samples - group * channels :],
        ("row", "col"),
        [(i, i + 1) for i in range(devices - 1)],
    )
    table = np.stack(interleaved_table(channels, group))
    frames_loc = samples // channels
    spectra_shape = (channels * 2 * group, frames_loc // group * inputs_loc)
    in_hbm = pl.BlockSpec(memory_space=pltpu.HBM)
    volt_early, taps, table, late = pl.pallas_call(
        later_kernel,
        out_shape=[
            jax.ShapeDtypeStruct((2, inputs_loc, group * channels), jnp.bfloat16),
            jax.ShapeDtypeStruct((fir_taps.shape[0], group * channels), jnp.float32),
            jax.ShapeDtypeStruct(table.shape, jnp.bfloat16),
            jax.ShapeDtypeStruct(spectra_shape, jnp.bfloat16),
        ],
        in_specs=[in_hbm] * 3,
        out_specs=[whole] * 4,
        scratch_shapes=[
            pltpu.VMEM(voltages.shape, jnp.bfloat16),
            pltpu.VMEM(fir_taps.shape, jnp.float32),
            pltpu.SemaphoreType.DMA((3,)),
        ],
        cost_estimate=pl.CostEstimate(flops=500_000_000, bytes_accessed=3_000_000, transcendentals=0),
        compiler_params=params,
        name="later_frames",
    )(voltages, fir_taps, jnp.asarray(table))
    spectra = pl.pallas_call(
        first_kernel,
        out_shape=jax.ShapeDtypeStruct(spectra_shape, jnp.bfloat16),
        in_specs=[whole] * 5,
        out_specs=whole,
        compiler_params=params,
        name="first_frames",
    )(volt_early, halo, taps, table, late)
    spectra = spectra.reshape(chan_size, -1, spectra.shape[1])
    turned = lax.all_to_all(spectra, "chan", split_axis=0, concat_axis=0, tiled=True)
    both = lax.all_gather(turned, "row", axis=0)

    half = chan_size * inputs_loc // row_size
    keep, give = pl.pallas_call(
        turn_kernel,
        out_shape=[jax.ShapeDtypeStruct((half, LANES), jnp.bfloat16)] * 2,
        in_specs=[whole],
        out_specs=[whole] * 2,
        compiler_params=params,
        name="turn",
    )(both)

    late = col_size // 2
    later, every = range(late, col_size), range(col_size)

    def pairs_of(distance, reach, wanted, up):
        core, sign = (0, 1) if up else (1, -1)
        hops = []
        for plane in range(col_size):
            if any((plane + sign * d) % col_size in wanted for d in range(distance, reach + 1)):
                source = (plane + sign * (distance - 1)) % col_size
                hops.append((core * col_size + source, core * col_size + (source + sign) % col_size))
        return hops

    def keep_on(array, distance):
        hops = pairs_of(distance, late, every, True) + pairs_of(distance, late, later, False)
        return lax.ppermute(array, ("row", "col"), hops)

    def give_on(array, distance):
        hops = pairs_of(distance, late - 1, later, True) + pairs_of(distance, late - 1, every, False)
        return lax.ppermute(array, ("row", "col"), hops)

    on_chip = lambda array: lax.all_gather(array, "row", axis=0)

    cols = chan_size * inputs_loc // col_size
    col_slice = lambda array, at: lax.dynamic_slice_in_dim(array, lax.rem(at, half // cols) * cols, cols, 0)
    keeps, gives = [keep], [give]
    for step in range(late - 1):
        keeps.append(keep_on(keeps[-1], step + 1))
        gives.append(give_on(gives[-1], step + 1))
    far = lax.ppermute(
        jnp.concatenate([col_slice(k, col + col_size - 1) for k in keeps], 0),
        ("row", "col"),
        [(col_size + (c + 1) % col_size, c) for c in later],
    )
    keeps.append(keep_on(keeps[-1], late))
    shared = [on_chip(g) for g in gives[1:]]

    tile = 256
    near = pl.pallas_call(
        near_columns_kernel,
        out_shape=jax.ShapeDtypeStruct((2, 2 * LANES, 2 * cols), jnp.bfloat16),
        in_specs=[whole] * 8,
        out_specs=whole,
        cost_estimate=pl.CostEstimate(flops=NEAR_FLOPS, bytes_accessed=1_500_000, transcendentals=0),
        compiler_params=params,
        name="near_columns",
    )(*keeps[:-1], *gives)
    operands = [*keeps, near, *shared, far]
    out_shape = (2, 2, half, cols)
    return pl.pallas_call(
        functools.partial(correlate_kernel, 1.0 / math.sqrt(frames_loc * devices), tile),
        out_shape=jax.ShapeDtypeStruct(out_shape, jnp.bfloat16),
        in_specs=[whole] * len(operands),
        out_specs=pl.BlockSpec(memory_space=pl.ANY),
        scratch_shapes=[
            pltpu.VMEM(out_shape, jnp.bfloat16),
            pltpu.VMEM((2, 2 * LANES, 2 * cols), jnp.bfloat16),
            pltpu.SemaphoreType.DMA((half // tile,)),
        ],
        compiler_params=params,
        name="correlate",
    )(*operands)


def solution(mesh):
    placed = (P(None, "chan", ("row", "col")), P())
    return jax.shard_map(
        shards, mesh=mesh, in_specs=placed, out_specs=P(None, "chan", "row", "col"), check_vma=False
    )
```

```python
import functools
import math

import jax
import jax.numpy as jnp
import numpy as np
from jax import lax
from jax.experimental import pallas as pl
from jax.experimental.pallas import tpu as pltpu
from jax.sharding import PartitionSpec as P

VMEM_LIMIT = 40 * 1024 * 1024
LANES = 128
NEAR_FLOPS = 4_000_000_000


def interleaved_table(channels, group):
    index = np.arange(channels)
    angle = (index[:, None] * index[None, :] % channels) * (2.0 * math.pi / channels)
    cosine, sine = np.cos(angle), np.sin(angle)
    dft = np.stack([np.stack([cosine, sine], 1), np.stack([-sine, cosine], 1)], 1)
    dft = dft / math.sqrt(channels)
    table = np.einsum("kopn,tu->kotpun", dft, np.eye(group))
    table = table.reshape(channels * 2 * group, 2 * group * channels).astype(np.float32)
    high = table.astype(jnp.bfloat16)
    return high, (table - high.astype(np.float32)).astype(jnp.bfloat16)


def product_nt(a, b):
    return lax.dot_general(a, b, (((1,), (1,)), ((), ())), preferred_element_type=jnp.float32)


def filtered_groups(extended, taps, head, width):
    samples = extended[0].shape[1] - head
    channels = LANES // 2
    parts = []
    for wide in extended:
        rolled = pltpu.roll(wide, channels, 1)
        parts.append(
            taps[0:1, :samples] * wide[:, head:]
            + taps[1:2, :samples] * rolled[:, head:]
            + taps[2:3, :samples] * wide[:, head - LANES : head - LANES + samples]
            + taps[3:4, :samples] * rolled[:, head - LANES : head - LANES + samples]
        )
    rows = [
        jnp.concatenate([p[:, start : start + width] for p in parts], 1) for start in range(0, samples, width)
    ]
    return jnp.concatenate(rows, 0)


def transformed(frames, high, rest):
    frames_high = frames.astype(jnp.bfloat16)
    frames_rest = (frames - frames_high.astype(jnp.float32)).astype(jnp.bfloat16)
    spectra = product_nt(high, frames_rest) + product_nt(rest, frames_high)
    return (spectra + product_nt(high, frames_high)).astype(jnp.bfloat16)


def reach_of(half_rows, cols):
    return (lax.axis_index("col") + 1) * cols - lax.axis_index("row") * half_rows


def later_kernel(
    tile_rows, volt_hbm, taps_hbm, table_hbm, volt_out, taps_out, table_out, late_out, vis_hbm, volt_ref, taps_ref, zero_ref, sems
):
    copies = [
        pltpu.make_async_copy(source, target, sems.at[i])
        for i, (source, target) in enumerate(
            ((volt_hbm, volt_ref), (taps_hbm, taps_ref), (table_hbm, table_out))
        )
    ]
    for copy in copies:
        copy.start()

    half_rows, cols = vis_hbm.shape[2:]
    reach = reach_of(half_rows, cols)
    starts = range(0, half_rows, tile_rows)
    zero_copies = [
        pltpu.make_async_copy(zero_ref, vis_hbm.at[:, :, start : start + tile_rows, :], sems.at[3 + i])
        for i, start in enumerate(starts)
    ]

    @pl.when(reach < half_rows)
    def _():
        zero_ref[...] = jnp.zeros(zero_ref.shape, zero_ref.dtype)

    for start, copy in zip(starts, zero_copies):
        pl.when(reach <= start)(copy.start)

    copies[0].wait()
    copies[1].wait()
    samples = volt_ref.shape[2]
    width = table_out.shape[2] // 2
    wide = jnp.concatenate([taps_ref[...]] * (LANES // taps_ref.shape[1]), 1)
    taps = jnp.concatenate([wide] * (samples // LANES), 1)
    taps_out[...] = taps[:, :width]
    volt_out[...] = volt_ref[:, :, :width]
    extended = [volt_ref[part].astype(jnp.float32) for part in range(2)]
    frames = filtered_groups(extended, taps, width, width)
    first = jnp.zeros((volt_ref.shape[1], frames.shape[1]), jnp.float32)
    copies[2].wait()
    late_out[...] = transformed(jnp.concatenate([first, frames], 0), table_out[0], table_out[1])
    for start, copy in zip(starts, zero_copies):
        pl.when(reach <= start)(copy.wait)


def first_kernel(volt_ref, halo_ref, taps_ref, table_ref, late_ref, out_ref):
    extended = [
        jnp.concatenate([halo_ref[part], volt_ref[part]], 1).astype(jnp.float32) for part in range(2)
    ]
    frames = filtered_groups(extended, taps_ref[...], halo_ref.shape[2], table_ref.shape[2] // 2)
    frames = jnp.concatenate([frames, jnp.zeros((LANES - frames.shape[0], frames.shape[1]), jnp.float32)], 0)
    first = transformed(frames, table_ref[0], table_ref[1])
    out_ref[:, :LANES] = first + late_ref[:, :LANES]
    out_ref[:, LANES:] = late_ref[:, LANES:]


def turn_kernel(in_ref, *out_refs):
    row, odd = lax.axis_index("row"), lax.axis_index("col") % 2 == 1
    pairs = in_ref.shape[1] // 4
    half_lanes = LANES // 2
    low = lax.broadcasted_iota(jnp.int32, (8, LANES), 1) < half_lanes
    for half, out_ref in zip((row, 1 - row), out_refs):
        for pair in range(pairs):
            first = [in_ref[r, half * 2 * pairs + 2 * pair].astype(jnp.float32) for r in range(2)]
            second = [in_ref[r, half * 2 * pairs + 2 * pair + 1].astype(jnp.float32) for r in range(2)]
            pieces = []
            for ch in range(2):
                for g in range(4):
                    for r in range(2):
                        tile = (slice(ch * 8, ch * 8 + 8), slice((g // 2) * LANES, (g // 2 + 1) * LANES))
                        a, b = first[r][tile], second[r][tile]
                        if g % 2 == 0:
                            pieces.append(jnp.where(low, a, pltpu.roll(b, half_lanes, 1)))
                        else:
                            pieces.append(jnp.where(low, pltpu.roll(a, half_lanes, 1), b))
            count = len(pieces) // 2
            block = jnp.concatenate(
                [jnp.where(odd, pieces[(i + count) % (2 * count)], pieces[i]) for i in range(2 * count)], 0
            )
            out_ref[pl.ds(pair * LANES, LANES), :] = block.T.astype(jnp.bfloat16)


def by_channel(one, other):
    low = lax.broadcasted_iota(jnp.int32, one.shape, 1) < LANES // 2
    return jnp.where(low, one, other), jnp.where(low, other, one)


def place_of_columns(cols, half_rows):
    row, col = lax.axis_index("row"), lax.axis_index("col")
    per_half = half_rows // cols
    at = pl.ds(pl.multiple_of((col % per_half) * cols, cols), cols)
    return row, col, at, (row == 0) & (col >= per_half)


def put_columns(one, other, right_ref, first_lane):
    cols = one.shape[0]
    target = lax.broadcasted_iota(jnp.int32, (LANES, LANES), 0)
    source = lax.broadcasted_iota(jnp.int32, (LANES, LANES), 1)
    same = (source == target).astype(jnp.bfloat16)
    turn = jnp.where(target == source + 4, 1.0, 0.0) * (source % 8 < 4).astype(jnp.float32)
    turn = turn - jnp.where(target == source - 4, 1.0, 0.0) * (source % 8 >= 4).astype(jnp.float32)
    turn = turn.astype(jnp.bfloat16)
    lanes = slice(first_lane, first_lane + LANES)
    for ch, block in enumerate(by_channel(one, other)):
        right_ref[ch, lanes, 0:cols] = product_nt(same, block).astype(jnp.bfloat16)
        right_ref[ch, lanes, cols : 2 * cols] = product_nt(turn, block).astype(jnp.bfloat16)


def for_tiles(half_rows, tile_rows, cols, prepare, products, finish=None):
    starts = range(0, half_rows, tile_rows)
    reach = reach_of(half_rows, cols)

    @pl.when(reach >= half_rows)
    def _():
        prepare()
        for start in starts:
            products(start)
        for start in starts if finish else ():
            finish(start)

    @pl.when((reach > 0) & (reach < half_rows))
    def _():
        prepare()
        for start in starts:
            pl.when(reach > start)(functools.partial(products, start))
        for start in starts if finish else ():
            pl.when(reach > start)(functools.partial(finish, start))


def near_kernel(tile_rows, k0, k1, k2, k3, g0, g1, g2, g3, sum_ref, right_ref):
    half_rows = k0.shape[0]
    cols = sum_ref.shape[2] // 2
    _, _, at, elsewhere = place_of_columns(cols, half_rows)

    def prepare():
        near = [jnp.where(elsewhere, g[at, :], k[at, :]) for k, g in ((k0, g0), (k1, g1), (k2, g2), (k3, g3))]
        put_columns(near[0], near[1], right_ref, 0)
        put_columns(near[2], near[3], right_ref, LANES)

    def products(start):
        here = slice(start, start + tile_rows)
        pairs = ((k0[here, :], k1[here, :]), (k2[here, :], k3[here, :]))
        split = [by_channel(*pair) for pair in pairs]
        for ch in range(2):
            left = jnp.concatenate([blocks[ch] for blocks in split], 1)
            sum_ref[ch, here, :] = jnp.dot(left, right_ref[ch], preferred_element_type=jnp.float32)

    for_tiles(half_rows, tile_rows, cols, prepare, products)


def correlate_kernel(scale, tile_rows, k4, s1, s2, s3, far, near, zeros_hbm, out_hbm, out_ref, right_ref, sems):
    half_rows = k4.shape[0]
    cols = out_ref.shape[3]
    row, col, at, elsewhere = place_of_columns(cols, half_rows)
    away = 1 - row
    odd = col % 2 == 1

    def prepare():
        four = jnp.where(elsewhere, far[3 * cols : 4 * cols, :], k4[at, :])
        three = jnp.where(elsewhere, far[2 * cols : 3 * cols, :], s3[away, at, :])
        put_columns(four, three, right_ref, 0)
        two = jnp.where(elsewhere, far[cols : 2 * cols, :], s2[away, at, :])
        one = jnp.where(elsewhere, far[0:cols, :], s1[away, at, :])
        put_columns(two, one, right_ref, LANES)

    def copy_of(start):
        here = slice(start, start + tile_rows)
        return pltpu.make_async_copy(
            out_ref.at[:, :, here, :], out_hbm.at[:, :, here, :], sems.at[start // tile_rows]
        )

    def products(start):
        here = slice(start, start + tile_rows)
        pairs = ((k4[here, :], s3[away, here, :]), (s2[away, here, :], s1[away, here, :]))
        split = [by_channel(*pair) for pair in pairs]
        row_ids = row * half_rows + start + lax.broadcasted_iota(jnp.int32, (tile_rows, cols), 0)
        col_ids = col * cols + lax.broadcasted_iota(jnp.int32, (tile_rows, cols), 1)
        upper = row_ids < col_ids
        for ch in range(2):
            left = jnp.concatenate([blocks[ch] for blocks in split], 1)
            total = jnp.dot(left, right_ref[ch], preferred_element_type=jnp.float32)
            total = (total + near[ch, here, :]) * scale
            goes_to = jnp.where(odd, 1 - ch, ch)
            out_ref[0, goes_to, here, :] = jnp.where(upper, total[:, :cols], 0.0).astype(jnp.bfloat16)
            out_ref[1, goes_to, here, :] = jnp.where(upper, total[:, cols:], 0.0).astype(jnp.bfloat16)
        copy_of(start).start()

    for_tiles(half_rows, tile_rows, cols, prepare, products, lambda start: copy_of(start).wait())


def shards(voltages, fir_taps):
    inputs_loc, samples = voltages.shape[1:]
    channels = fir_taps.shape[1]
    group = 4
    chan_size, row_size, col_size = (lax.axis_size(a) for a in ("chan", "row", "col"))
    row, col = lax.axis_index("row"), lax.axis_index("col")
    devices = row_size * col_size
    params = pltpu.CompilerParams(vmem_limit_bytes=VMEM_LIMIT)
    whole = pl.BlockSpec(memory_space=pltpu.VMEM)

    halo = lax.ppermute(
        voltages[:, :, samples - group * channels :],
        ("row", "col"),
        [(i, i + 1) for i in range(devices - 1)],
    )
    table = np.stack(interleaved_table(channels, group))
    frames_loc = samples // channels
    spectra_shape = (channels * 2 * group, frames_loc // group * inputs_loc)
    in_hbm = pl.BlockSpec(memory_space=pltpu.HBM)
    tile = 256
    half = chan_size * inputs_loc // row_size
    cols = chan_size * inputs_loc // col_size
    vis_shape = jax.ShapeDtypeStruct((2, 2, half, cols), jnp.bfloat16)
    volt_early, taps, table, late, visibilities = pl.pallas_call(
        functools.partial(later_kernel, tile),
        out_shape=[
            jax.ShapeDtypeStruct((2, inputs_loc, group * channels), jnp.bfloat16),
            jax.ShapeDtypeStruct((fir_taps.shape[0], group * channels), jnp.float32),
            jax.ShapeDtypeStruct(table.shape, jnp.bfloat16),
            jax.ShapeDtypeStruct(spectra_shape, jnp.bfloat16),
            vis_shape,
        ],
        in_specs=[in_hbm] * 3,
        out_specs=[whole] * 4 + [pl.BlockSpec(memory_space=pl.ANY)],
        scratch_shapes=[
            pltpu.VMEM(voltages.shape, jnp.bfloat16),
            pltpu.VMEM(fir_taps.shape, jnp.float32),
            pltpu.VMEM((2, 2, tile, cols), jnp.bfloat16),
            pltpu.SemaphoreType.DMA((3 + half // tile,)),
        ],
        cost_estimate=pl.CostEstimate(flops=500_000_000, bytes_accessed=3_000_000, transcendentals=0),
        compiler_params=params,
        name="later_frames",
    )(voltages, fir_taps, jnp.asarray(table))
    spectra = pl.pallas_call(
        first_kernel,
        out_shape=jax.ShapeDtypeStruct(spectra_shape, jnp.bfloat16),
        in_specs=[whole] * 5,
        out_specs=whole,
        compiler_params=params,
        name="first_frames",
    )(volt_early, halo, taps, table, late)
    spectra = spectra.reshape(chan_size, -1, spectra.shape[1])
    turned = lax.all_to_all(spectra, "chan", split_axis=0, concat_axis=0, tiled=True)
    both = lax.all_gather(turned, "row", axis=0)

    keep, give = pl.pallas_call(
        turn_kernel,
        out_shape=[jax.ShapeDtypeStruct((half, LANES), jnp.bfloat16)] * 2,
        in_specs=[whole],
        out_specs=[whole] * 2,
        compiler_params=params,
        name="turn",
    )(both)

    late = col_size // 2
    later, every = range(late, col_size), range(col_size)

    def pairs_of(distance, reach, wanted, up):
        core, sign = (0, 1) if up else (1, -1)
        hops = []
        for plane in range(col_size):
            if any((plane + sign * d) % col_size in wanted for d in range(distance, reach + 1)):
                source = (plane + sign * (distance - 1)) % col_size
                hops.append((core * col_size + source, core * col_size + (source + sign) % col_size))
        return hops

    def keep_on(array, distance):
        hops = pairs_of(distance, late, every, True) + pairs_of(distance, late, later, False)
        return lax.ppermute(array, ("row", "col"), hops)

    def give_on(array, distance):
        hops = pairs_of(distance, late - 1, later, True) + pairs_of(distance, late - 1, every, False)
        return lax.ppermute(array, ("row", "col"), hops)

    on_chip = lambda array: lax.all_gather(array, "row", axis=0)

    col_slice = lambda array, at: lax.dynamic_slice_in_dim(array, lax.rem(at, half // cols) * cols, cols, 0)
    keeps, gives = [keep], [give]
    for step in range(late - 1):
        keeps.append(keep_on(keeps[-1], step + 1))
        gives.append(give_on(gives[-1], step + 1))
    far = lax.ppermute(
        jnp.concatenate([col_slice(k, col + col_size - 1) for k in keeps], 0),
        ("row", "col"),
        [(col_size + (c + 1) % col_size, c) for c in later],
    )
    keeps.append(keep_on(keeps[-1], late))
    shared = [on_chip(g) for g in gives[1:]]

    near = pl.pallas_call(
        functools.partial(near_kernel, tile),
        out_shape=jax.ShapeDtypeStruct((2, half, 2 * cols), jnp.float32),
        in_specs=[whole] * 8,
        out_specs=whole,
        scratch_shapes=[pltpu.VMEM((2, 2 * LANES, 2 * cols), jnp.bfloat16)],
        cost_estimate=pl.CostEstimate(flops=NEAR_FLOPS, bytes_accessed=6_000_000, transcendentals=0),
        compiler_params=params,
        name="near_planes",
    )(*keeps[:-1], *gives)
    return pl.pallas_call(
        functools.partial(correlate_kernel, 1.0 / math.sqrt(frames_loc * devices), tile),
        out_shape=vis_shape,
        in_specs=[whole] * 6 + [pl.BlockSpec(memory_space=pl.ANY)],
        out_specs=pl.BlockSpec(memory_space=pl.ANY),
        input_output_aliases={6: 0},
        scratch_shapes=[
            pltpu.VMEM(vis_shape.shape, jnp.bfloat16),
            pltpu.VMEM((2, 2 * LANES, 2 * cols), jnp.bfloat16),
            pltpu.SemaphoreType.DMA((half // tile,)),
        ],
        compiler_params=params,
        name="correlate",
    )(keeps[-1], *shared, far, near, visibilities)


def solution(mesh):
    placed = (P(None, "chan", ("row", "col")), P())
    return jax.shard_map(
        shards, mesh=mesh, in_specs=placed, out_specs=P(None, "chan", "row", "col"), check_vma=False
    )
```

```python
import functools
import math

import jax
import jax.numpy as jnp
import numpy as np
from jax import lax
from jax.experimental import pallas as pl
from jax.experimental.pallas import tpu as pltpu
from jax.sharding import PartitionSpec as P

VMEM_LIMIT = 40 * 1024 * 1024
LANES = 128
NEAR_FLOPS = 4_000_000_000


def interleaved_table(channels, group):
    index = np.arange(channels)
    angle = (index[:, None] * index[None, :] % channels) * (2.0 * math.pi / channels)
    cosine, sine = np.cos(angle), np.sin(angle)
    dft = np.stack([np.stack([cosine, sine], 1), np.stack([-sine, cosine], 1)], 1)
    dft = dft / math.sqrt(channels)
    table = np.einsum("kopn,tu->kotpun", dft, np.eye(group))
    table = table.reshape(channels * 2 * group, 2 * group * channels).astype(np.float32)
    high = table.astype(jnp.bfloat16)
    return high, (table - high.astype(np.float32)).astype(jnp.bfloat16)


def product_nt(a, b):
    return lax.dot_general(a, b, (((1,), (1,)), ((), ())), preferred_element_type=jnp.float32)


def filtered_groups(extended, taps, head, width):
    samples = extended[0].shape[1] - head
    channels = LANES // 2
    parts = []
    for wide in extended:
        rolled = pltpu.roll(wide, channels, 1)
        parts.append(
            taps[0:1, :samples] * wide[:, head:]
            + taps[1:2, :samples] * rolled[:, head:]
            + taps[2:3, :samples] * wide[:, head - LANES : head - LANES + samples]
            + taps[3:4, :samples] * rolled[:, head - LANES : head - LANES + samples]
        )
    rows = [
        jnp.concatenate([p[:, start : start + width] for p in parts], 1) for start in range(0, samples, width)
    ]
    return jnp.concatenate(rows, 0)


def transformed(frames, high, rest):
    frames_high = frames.astype(jnp.bfloat16)
    frames_rest = (frames - frames_high.astype(jnp.float32)).astype(jnp.bfloat16)
    spectra = product_nt(high, frames_rest) + product_nt(rest, frames_high)
    return (spectra + product_nt(high, frames_high)).astype(jnp.bfloat16)


def reach_of(half_rows, cols):
    return (lax.axis_index("col") + 1) * cols - lax.axis_index("row") * half_rows


def later_kernel(
    tile_rows, volt_hbm, taps_hbm, table_hbm, volt_out, taps_out, table_out, late_out, vis_hbm, volt_ref, taps_ref, zero_ref, sems
):
    copies = [
        pltpu.make_async_copy(source, target, sems.at[i])
        for i, (source, target) in enumerate(
            ((volt_hbm, volt_ref), (taps_hbm, taps_ref), (table_hbm, table_out))
        )
    ]
    for copy in copies:
        copy.start()

    half_rows, cols = vis_hbm.shape[2:]
    reach = reach_of(half_rows, cols)
    starts = range(0, half_rows, tile_rows)
    zero_copies = [
        pltpu.make_async_copy(zero_ref, vis_hbm.at[:, :, start : start + tile_rows, :], sems.at[3 + i])
        for i, start in enumerate(starts)
    ]

    @pl.when(reach < half_rows)
    def _():
        zero_ref[...] = jnp.zeros(zero_ref.shape, zero_ref.dtype)

    for start, copy in zip(starts, zero_copies):
        pl.when(reach <= start)(copy.start)

    copies[0].wait()
    copies[1].wait()
    samples = volt_ref.shape[2]
    width = table_out.shape[2] // 2
    wide = jnp.concatenate([taps_ref[...]] * (LANES // taps_ref.shape[1]), 1)
    taps = jnp.concatenate([wide] * (samples // LANES), 1)
    taps_out[...] = taps[:, :width]
    volt_out[...] = volt_ref[:, :, :width]
    extended = [volt_ref[part].astype(jnp.float32) for part in range(2)]
    frames = filtered_groups(extended, taps, width, width)
    first = jnp.zeros((volt_ref.shape[1], frames.shape[1]), jnp.float32)
    copies[2].wait()
    late_out[...] = transformed(jnp.concatenate([first, frames], 0), table_out[0], table_out[1])
    for start, copy in zip(starts, zero_copies):
        pl.when(reach <= start)(copy.wait)


def first_kernel(volt_ref, halo_ref, taps_ref, table_ref, late_ref, out_ref):
    extended = [
        jnp.concatenate([halo_ref[part], volt_ref[part]], 1).astype(jnp.float32) for part in range(2)
    ]
    frames = filtered_groups(extended, taps_ref[...], halo_ref.shape[2], table_ref.shape[2] // 2)
    frames = jnp.concatenate([frames, jnp.zeros((LANES - frames.shape[0], frames.shape[1]), jnp.float32)], 0)
    first = transformed(frames, table_ref[0], table_ref[1])
    out_ref[:, :LANES] = first + late_ref[:, :LANES]
    out_ref[:, LANES:] = late_ref[:, LANES:]


def turn_kernel(in_ref, *out_refs):
    row, odd = lax.axis_index("row"), lax.axis_index("col") % 2 == 1
    pairs = in_ref.shape[1] // 4
    half_lanes = LANES // 2
    low = lax.broadcasted_iota(jnp.int32, (8, LANES), 1) < half_lanes
    for half, out_ref in zip((row, 1 - row), out_refs):
        for pair in range(pairs):
            first = [in_ref[r, half * 2 * pairs + 2 * pair].astype(jnp.float32) for r in range(2)]
            second = [in_ref[r, half * 2 * pairs + 2 * pair + 1].astype(jnp.float32) for r in range(2)]
            pieces = []
            for ch in range(2):
                for g in range(4):
                    for r in range(2):
                        tile = (slice(ch * 8, ch * 8 + 8), slice((g // 2) * LANES, (g // 2 + 1) * LANES))
                        a, b = first[r][tile], second[r][tile]
                        if g % 2 == 0:
                            pieces.append(jnp.where(low, a, pltpu.roll(b, half_lanes, 1)))
                        else:
                            pieces.append(jnp.where(low, pltpu.roll(a, half_lanes, 1), b))
            count = len(pieces) // 2
            block = jnp.concatenate(
                [jnp.where(odd, pieces[(i + count) % (2 * count)], pieces[i]) for i in range(2 * count)], 0
            )
            out_ref[pl.ds(pair * LANES, LANES), :] = block.T.astype(jnp.bfloat16)


def by_channel(one, other):
    low = lax.broadcasted_iota(jnp.int32, one.shape, 1) < LANES // 2
    return jnp.where(low, one, other), jnp.where(low, other, one)


def place_of_columns(cols, half_rows):
    row, col = lax.axis_index("row"), lax.axis_index("col")
    per_half = half_rows // cols
    at = pl.ds(pl.multiple_of((col % per_half) * cols, cols), cols)
    return row, col, at, (row == 0) & (col >= per_half)


def put_columns(one, other, right_ref, first_lane):
    cols = one.shape[0]
    target = lax.broadcasted_iota(jnp.int32, (LANES, LANES), 0)
    source = lax.broadcasted_iota(jnp.int32, (LANES, LANES), 1)
    same = (source == target).astype(jnp.bfloat16)
    turn = jnp.where(target == source + 4, 1.0, 0.0) * (source % 8 < 4).astype(jnp.float32)
    turn = turn - jnp.where(target == source - 4, 1.0, 0.0) * (source % 8 >= 4).astype(jnp.float32)
    turn = turn.astype(jnp.bfloat16)
    lanes = slice(first_lane, first_lane + LANES)
    for ch, block in enumerate(by_channel(one, other)):
        right_ref[ch, lanes, 0:cols] = product_nt(same, block).astype(jnp.bfloat16)
        right_ref[ch, lanes, cols : 2 * cols] = product_nt(turn, block).astype(jnp.bfloat16)


def for_tiles(half_rows, tile_rows, cols, prepare, products, finish=None):
    starts = range(0, half_rows, tile_rows)
    reach = reach_of(half_rows, cols)

    @pl.when(reach >= half_rows)
    def _():
        prepare()
        for start in starts:
            products(start)
        for start in starts if finish else ():
            finish(start)

    @pl.when((reach > 0) & (reach < half_rows))
    def _():
        prepare()
        for start in starts:
            pl.when(reach > start)(functools.partial(products, start))
        for start in starts if finish else ():
            pl.when(reach > start)(functools.partial(finish, start))


def near_kernel(tile_rows, k0, k1, k2, k3, g0, g1, g2, g3, sum_ref, right_ref):
    half_rows = k0.shape[0]
    cols = sum_ref.shape[2] // 2
    _, _, at, elsewhere = place_of_columns(cols, half_rows)

    def prepare():
        near = [jnp.where(elsewhere, g[at, :], k[at, :]) for k, g in ((k0, g0), (k1, g1), (k2, g2), (k3, g3))]
        put_columns(near[0], near[1], right_ref, 0)
        put_columns(near[2], near[3], right_ref, LANES)

    def products(start):
        here = slice(start, start + tile_rows)
        pairs = ((k0[here, :], k1[here, :]), (k2[here, :], k3[here, :]))
        split = [by_channel(*pair) for pair in pairs]
        for ch in range(2):
            left = jnp.concatenate([blocks[ch] for blocks in split], 1)
            sum_ref[ch, here, :] = jnp.dot(left, right_ref[ch], preferred_element_type=jnp.float32)

    for_tiles(half_rows, tile_rows, cols, prepare, products)


def correlate_kernel(scale, tile_rows, k4, s1, s2, s3, far, near, zeros_hbm, out_hbm, out_ref, right_ref, sems):
    half_rows = k4.shape[0]
    cols = out_ref.shape[3]
    row, col, at, elsewhere = place_of_columns(cols, half_rows)
    away = 1 - row
    odd = col % 2 == 1

    def prepare():
        four = jnp.where(elsewhere, far[3 * cols : 4 * cols, :], k4[at, :])
        three = jnp.where(elsewhere, far[2 * cols : 3 * cols, :], s3[away, at, :])
        put_columns(four, three, right_ref, 0)
        two = jnp.where(elsewhere, far[cols : 2 * cols, :], s2[away, at, :])
        one = jnp.where(elsewhere, far[0:cols, :], s1[away, at, :])
        put_columns(two, one, right_ref, LANES)

    def copy_of(start, ch):
        here = slice(start, start + tile_rows)
        goes_to = jnp.where(odd, 1 - ch, ch)
        return pltpu.make_async_copy(
            out_ref.at[:, goes_to, here, :], out_hbm.at[:, goes_to, here, :], sems.at[start // tile_rows, ch]
        )

    def finish(start):
        for ch in range(2):
            copy_of(start, ch).wait()

    def products(start):
        here = slice(start, start + tile_rows)
        pairs = ((k4[here, :], s3[away, here, :]), (s2[away, here, :], s1[away, here, :]))
        split = [by_channel(*pair) for pair in pairs]
        row_ids = row * half_rows + start + lax.broadcasted_iota(jnp.int32, (tile_rows, cols), 0)
        col_ids = col * cols + lax.broadcasted_iota(jnp.int32, (tile_rows, cols), 1)
        upper = row_ids < col_ids
        for ch in range(2):
            left = jnp.concatenate([blocks[ch] for blocks in split], 1)
            total = jnp.dot(left, right_ref[ch], preferred_element_type=jnp.float32)
            total = (total + near[ch, here, :]) * scale
            goes_to = jnp.where(odd, 1 - ch, ch)
            out_ref[0, goes_to, here, :] = jnp.where(upper, total[:, :cols], 0.0).astype(jnp.bfloat16)
            out_ref[1, goes_to, here, :] = jnp.where(upper, total[:, cols:], 0.0).astype(jnp.bfloat16)
            copy_of(start, ch).start()

    for_tiles(half_rows, tile_rows, cols, prepare, products, finish)


def shards(voltages, fir_taps):
    inputs_loc, samples = voltages.shape[1:]
    channels = fir_taps.shape[1]
    group = 4
    chan_size, row_size, col_size = (lax.axis_size(a) for a in ("chan", "row", "col"))
    row, col = lax.axis_index("row"), lax.axis_index("col")
    devices = row_size * col_size
    params = pltpu.CompilerParams(vmem_limit_bytes=VMEM_LIMIT)
    whole = pl.BlockSpec(memory_space=pltpu.VMEM)

    halo = lax.ppermute(
        voltages[:, :, samples - group * channels :],
        ("row", "col"),
        [(i, i + 1) for i in range(devices - 1)],
    )
    table = np.stack(interleaved_table(channels, group))
    frames_loc = samples // channels
    spectra_shape = (channels * 2 * group, frames_loc // group * inputs_loc)
    in_hbm = pl.BlockSpec(memory_space=pltpu.HBM)
    tile = 256
    half = chan_size * inputs_loc // row_size
    cols = chan_size * inputs_loc // col_size
    vis_shape = jax.ShapeDtypeStruct((2, 2, half, cols), jnp.bfloat16)
    volt_early, taps, table, late, visibilities = pl.pallas_call(
        functools.partial(later_kernel, tile),
        out_shape=[
            jax.ShapeDtypeStruct((2, inputs_loc, group * channels), jnp.bfloat16),
            jax.ShapeDtypeStruct((fir_taps.shape[0], group * channels), jnp.float32),
            jax.ShapeDtypeStruct(table.shape, jnp.bfloat16),
            jax.ShapeDtypeStruct(spectra_shape, jnp.bfloat16),
            vis_shape,
        ],
        in_specs=[in_hbm] * 3,
        out_specs=[whole] * 4 + [pl.BlockSpec(memory_space=pl.ANY)],
        scratch_shapes=[
            pltpu.VMEM(voltages.shape, jnp.bfloat16),
            pltpu.VMEM(fir_taps.shape, jnp.float32),
            pltpu.VMEM((2, 2, tile, cols), jnp.bfloat16),
            pltpu.SemaphoreType.DMA((3 + half // tile,)),
        ],
        cost_estimate=pl.CostEstimate(flops=500_000_000, bytes_accessed=3_000_000, transcendentals=0),
        compiler_params=params,
        name="later_frames",
    )(voltages, fir_taps, jnp.asarray(table))
    spectra = pl.pallas_call(
        first_kernel,
        out_shape=jax.ShapeDtypeStruct(spectra_shape, jnp.bfloat16),
        in_specs=[whole] * 5,
        out_specs=whole,
        compiler_params=params,
        name="first_frames",
    )(volt_early, halo, taps, table, late)
    spectra = spectra.reshape(chan_size, -1, spectra.shape[1])
    turned = lax.all_to_all(spectra, "chan", split_axis=0, concat_axis=0, tiled=True)
    both = lax.all_gather(turned, "row", axis=0)

    keep, give = pl.pallas_call(
        turn_kernel,
        out_shape=[jax.ShapeDtypeStruct((half, LANES), jnp.bfloat16)] * 2,
        in_specs=[whole],
        out_specs=[whole] * 2,
        compiler_params=params,
        name="turn",
    )(both)

    late = col_size // 2
    later, every = range(late, col_size), range(col_size)

    def pairs_of(distance, reach, wanted, up):
        core, sign = (0, 1) if up else (1, -1)
        hops = []
        for plane in range(col_size):
            if any((plane + sign * d) % col_size in wanted for d in range(distance, reach + 1)):
                source = (plane + sign * (distance - 1)) % col_size
                hops.append((core * col_size + source, core * col_size + (source + sign) % col_size))
        return hops

    def keep_on(array, distance):
        hops = pairs_of(distance, late, every, True) + pairs_of(distance, late, later, False)
        return lax.ppermute(array, ("row", "col"), hops)

    def give_on(array, distance):
        hops = pairs_of(distance, late - 1, later, True) + pairs_of(distance, late - 1, every, False)
        return lax.ppermute(array, ("row", "col"), hops)

    on_chip = lambda array: lax.all_gather(array, "row", axis=0)

    col_slice = lambda array, at: lax.dynamic_slice_in_dim(array, lax.rem(at, half // cols) * cols, cols, 0)
    keeps, gives = [keep], [give]
    for step in range(late - 1):
        keeps.append(keep_on(keeps[-1], step + 1))
        gives.append(give_on(gives[-1], step + 1))
    far = lax.ppermute(
        jnp.concatenate([col_slice(k, col + col_size - 1) for k in keeps], 0),
        ("row", "col"),
        [(col_size + (c + 1) % col_size, c) for c in later],
    )
    keeps.append(keep_on(keeps[-1], late))
    shared = [on_chip(g) for g in gives[1:]]

    near = pl.pallas_call(
        functools.partial(near_kernel, tile),
        out_shape=jax.ShapeDtypeStruct((2, half, 2 * cols), jnp.float32),
        in_specs=[whole] * 8,
        out_specs=whole,
        scratch_shapes=[pltpu.VMEM((2, 2 * LANES, 2 * cols), jnp.bfloat16)],
        cost_estimate=pl.CostEstimate(flops=NEAR_FLOPS, bytes_accessed=6_000_000, transcendentals=0),
        compiler_params=params,
        name="near_planes",
    )(*keeps[:-1], *gives)
    return pl.pallas_call(
        functools.partial(correlate_kernel, 1.0 / math.sqrt(frames_loc * devices), tile),
        out_shape=vis_shape,
        in_specs=[whole] * 6 + [pl.BlockSpec(memory_space=pl.ANY)],
        out_specs=pl.BlockSpec(memory_space=pl.ANY),
        input_output_aliases={6: 0},
        scratch_shapes=[
            pltpu.VMEM(vis_shape.shape, jnp.bfloat16),
            pltpu.VMEM((2, 2 * LANES, 2 * cols), jnp.bfloat16),
            pltpu.SemaphoreType.DMA((half // tile, 2)),
        ],
        compiler_params=params,
        name="correlate",
    )(keeps[-1], *shared, far, near, visibilities)


def solution(mesh):
    placed = (P(None, "chan", ("row", "col")), P())
    return jax.shard_map(
        shards, mesh=mesh, in_specs=placed, out_specs=P(None, "chan", "row", "col"), check_vma=False
    )
```
